256 devices in a mesh: ctx: 32 (over z, y_lo, core), head: 8 (over x, y_hi).
Axes of the slice: x: 4, y: 4 (y_hi: 2, y_lo: 2; y = y_hi * 2 + y_lo), z: 8, core: 2. Of those that a mesh axis runs over, the one named last changes fastest.
Arguments:
- queries: bfloat16 [8192, 8192], P(('ctx', 'head')), may hold values from -8 to 8
- keys: bfloat16 [8192, 1024], P(('ctx', 'head')), may hold values from -8 to 8
- values: bfloat16 [8192, 1024], P(('ctx', 'head')), may hold values from -3 to 3
- out_grad: bfloat16 [8192, 8192], P(('ctx', 'head')), may hold values from -3 to 3
- doc_ids: int32 [8192], replicated, may hold values from 0 to 31, never falling along the last dimension, each value on 1 to 4096 neighbouring positions
- block_order: int32 [64], replicated, may hold values from 0 to 63, each once
Outputs:
- attended: bfloat16 [8192, 8192], P(('ctx', 'head'))
- query_grad: bfloat16 [8192, 8192], P(('ctx', 'head'))
- key_grad: bfloat16 [8192, 1024], P(('ctx', 'head'))
- value_grad: bfloat16 [8192, 1024], P(('ctx', 'head'))
The draws below stay inside these ranges and needn't reach their ends.
Inputs may be any that keep to these rules, and one draw needn't show every extreme that they name: `doc_ids`: documents are numbered in packed order, each one contiguous. `block_order`: each block once.
All inputs are finite; a program needn't handle non-finite values.
Results may differ from the reference program's by a relative error of at most 0.038.
Values may be sent and summed in bfloat16 or wider, within the bound.
A program may use at most 64 MiB of HBM per device.

```python
import math
import jax
import jax.numpy as jnp
import numpy as np
from jax import lax

QH = 64
KVH = 8
HD = 128
BLK = 128
TOKENS = 8192
NBLK = 64
N_CTX = 32


def draw_queries(key, part):
    key = jax.random.fold_in(key, 11)
    base = jax.random.truncated_normal(key, -4.0, 4.0, (TOKENS, QH * HD), jnp.float32)
    return base.astype(jnp.bfloat16)


def draw_keys(key, part):
    key = jax.random.fold_in(key, 23)
    base = jax.random.truncated_normal(key, -4.0, 4.0, (TOKENS, KVH * HD), jnp.float32)
    return base.astype(jnp.bfloat16)


def level_of(own_key, extent, cuts, low, largest):
    level = 1.0
    for dim, parts in cuts:
        steps = jax.random.uniform(jax.random.fold_in(jax.random.fold_in(own_key, 6), dim), (parts,), jnp.float32, low / len(cuts), largest / len(cuts))
        level = level * jnp.repeat(jnp.exp(steps), extent[dim] // parts).reshape((-1,) + (1,) * (len(extent) - 1 - dim))
    return level


def profile(count, total, most, lean):
    loads = [(1 << 20) // math.isqrt(grade ** lean) + 1 for grade in range(2, count + 1)]
    surplus, counts = total - most - (count - 1), [1] * (count - 1)
    while surplus > 0:
        movable = [i for i in range(count - 1) if counts[i] < most]
        pool, left = sum([loads[i] for i in movable]), surplus
        for i in movable:
            addition = min(most - counts[i], max(1, left * loads[i] // pool), surplus)
            counts[i] = counts[i] + addition
            surplus = surplus - addition
    return np.array([most] + counts)


def ragged_sizes(rng, number_of, total, limit, lean):
    if number_of == 2:
        one = jax.random.randint(rng, (), max(1, total - limit), min(limit, total - 1) + 1)
        return jnp.stack([one, total - one])
    tallies = jnp.asarray(profile(number_of, total, limit, lean), jnp.int32)
    pairs = (number_of - 1) // 2
    giver, sink = tallies[1:1 + 2 * pairs:2], tallies[2:2 + 2 * pairs:2]
    room = jnp.minimum(giver - 1, limit - sink)
    moved = jax.random.randint(jax.random.fold_in(rng, 1), (pairs,), 0, 1 << 20) % (room + 1)
    tallies = tallies.at[1:1 + 2 * pairs:2].set(giver - moved).at[2:2 + 2 * pairs:2].set(sink + moved)
    return tallies[jax.random.permutation(jax.random.fold_in(rng, 2), number_of)]


def normal_values(own_key, extent, scale, bound, shards=(), held_as=jnp.bfloat16):
    factor_of = level_of(own_key, extent, shards, -0.22, 0.18) if shards else 1.0
    array = jax.random.normal(own_key, extent, jnp.float32) * scale * factor_of
    return jnp.minimum(jnp.maximum(array, -bound), bound).astype(held_as)


def setup_inputs(seed: int = 0) -> dict:
    key_list = jax.random.split(jax.random.key(seed), 7)
    queries = draw_queries(jax.random.fold_in(key_list[6], 71), 0)
    keys = draw_keys(jax.random.fold_in(key_list[6], 71), 0)
    values = normal_values(key_list[2], (TOKENS, KVH * HD), 0.5, 3.0, ((0, 256),))
    out_grad = normal_values(key_list[3], (TOKENS, QH * HD), 0.5, 3.0, ((0, 256),))
    doc_ids = jnp.searchsorted(jnp.cumsum(ragged_sizes(key_list[4], N_CTX, TOKENS, TOKENS // 2, 2)), jnp.arange(TOKENS), side="right").astype(jnp.int32)
    block_order = jax.random.permutation(key_list[5], NBLK).astype(jnp.int32)
    return dict(queries=queries, keys=keys, values=values, out_grad=out_grad, doc_ids=doc_ids, block_order=block_order)


def token_layout(doc_ids, block_order):
    index = jnp.arange(TOKENS, dtype=jnp.int32)
    place = block_order[index // BLK] * BLK + index % BLK
    return (place, doc_ids[place])

def reference(queries, keys, values, out_grad, doc_ids, block_order):
    scale = 1.0 / math.sqrt(HD)
    repeat = QH // KVH
    place, doc = token_layout(doc_ids, block_order)
    step_rows = math.gcd(TOKENS, 512)
    nsteps = TOKENS // step_rows
    query_heads = queries.reshape(TOKENS, KVH, repeat, HD).transpose(1, 0, 2, 3)
    grad_heads = out_grad.reshape(TOKENS, KVH, repeat, HD).transpose(1, 0, 2, 3)
    key_heads = keys.reshape(TOKENS, KVH, HD).transpose(1, 0, 2)
    value_heads = values.reshape(TOKENS, KVH, HD).transpose(1, 0, 2)

    def one_group(operands):
        qgrp, ggrp, kgrp, vgrp = operands
        kf = kgrp.astype(jnp.float32)
        vf = vgrp.astype(jnp.float32)

        def block(carry, index):
            dk_sum, dv_sum = carry
            start = index * step_rows
            qblk = lax.dynamic_slice_in_dim(qgrp, start, step_rows, 0).astype(jnp.float32)
            gblk = lax.dynamic_slice_in_dim(ggrp, start, step_rows, 0).astype(jnp.float32)
            qplace = lax.dynamic_slice_in_dim(place, start, step_rows, 0)
            qdoc = lax.dynamic_slice_in_dim(doc, start, step_rows, 0)
            visible = (qdoc[:, None] == doc[None, :]) & (place[None, :] <= qplace[:, None])
            score = jnp.einsum('qrd,kd->rqk', qblk, kf) * scale
            score = jnp.where(visible[None], score, -jnp.inf)
            top = lax.optimization_barrier(jnp.max(score, axis=-1, keepdims=True))
            lse = top + jnp.log(lax.optimization_barrier(jnp.sum(jnp.exp(score - top), axis=-1, keepdims=True)))
            prob = jnp.exp(score - lse).astype(jnp.bfloat16)
            probf = prob.astype(jnp.float32)
            attended = jnp.einsum('rqk,kd->qrd', probf, vf).astype(jnp.bfloat16)
            delta = lax.optimization_barrier(jnp.sum(gblk * attended.astype(jnp.float32), axis=-1))
            dprob = jnp.einsum('qrd,kd->rqk', gblk, vf)
            dscore = (probf * (dprob - delta.T[:, :, None])).astype(jnp.bfloat16).astype(jnp.float32)
            qgrad = (jnp.einsum('rqk,kd->qrd', dscore, kf) * scale).astype(jnp.bfloat16)
            dk_sum = dk_sum + jnp.einsum('rqk,qrd->kd', dscore, qblk)
            dv_sum = dv_sum + jnp.einsum('rqk,qrd->kd', probf, gblk)
            return ((dk_sum, dv_sum), (attended, qgrad))
        zero = jnp.zeros((TOKENS, HD), jnp.float32)
        (dk_sum, dv_sum), (att, qg) = lax.scan(block, (zero, zero), jnp.arange(nsteps, dtype=jnp.int32))
        att = att.reshape(TOKENS, repeat, HD)
        qg = qg.reshape(TOKENS, repeat, HD)
        return (att, qg, (dk_sum * scale).astype(jnp.bfloat16), dv_sum.astype(jnp.bfloat16))
    att, qg, kg, vg = lax.map(one_group, (query_heads, grad_heads, key_heads, value_heads))
    attended = att.transpose(1, 0, 2, 3).reshape(TOKENS, QH * HD)
    query_grad = qg.transpose(1, 0, 2, 3).reshape(TOKENS, QH * HD)
    key_grad = kg.transpose(1, 0, 2).reshape(TOKENS, KVH * HD)
    value_grad = vg.transpose(1, 0, 2).reshape(TOKENS, KVH * HD)
    return (attended, query_grad, key_grad, value_grad)
```

```python
import functools
import math

import jax
import jax.numpy as jnp
from jax import lax
from jax.experimental import pallas as pl
from jax.experimental.pallas import tpu as pltpu
from jax.sharding import PartitionSpec as P

QH = 64
KVH = 8
HD = 128
BLK = 128
NS = 4
KTILE = 512
LOG2E = math.log2(math.e)
SCALE = 1.0 / math.sqrt(HD)
NEG = -1e30
MESH = pl.DeviceIdType.MESH
F32 = jnp.float32
BF16 = jnp.bfloat16
NT = (((1,), (1,)), ((), ()))
NN = (((1,), (0,)), ((), ()))
VMEM_LIMIT = 56 * 1024 * 1024


def dot(a, b, dims):
    return lax.dot_general(a, b, dims, preferred_element_type=F32)


class Where:
    def __init__(self, planes, groups):
        ctx = lax.axis_index("ctx")
        self.planes, self.groups = planes, groups
        self.size = NS * groups
        self.g = lax.axis_index("head")
        self.z, self.s = ctx // NS, ctx % NS
        self.core, self.ylo = self.s % 2, self.s // 2
        self.p = self.s * groups + self.g
        self.up = (((self.z + 1) % planes) * NS + self.s, self.g)
        self.down = (((self.z + planes - 1) % planes) * NS + self.s, self.g)
        self.sib = (ctx + 1 - 2 * self.core, self.g)

    def peer(self, i):
        o = (self.p + i) % self.size
        return o, o // self.groups, o % self.groups, (self.z * NS + o // self.groups, o % self.groups)

    def greet(self):
        bar = pltpu.get_barrier_semaphore()

        def signal(i, carry):
            pl.semaphore_signal(bar, inc=1, device_id=self.peer(i)[3], device_id_type=MESH)
            return carry

        lax.fori_loop(1, self.size, signal, 0)
        for other in (self.up, self.down):
            pl.semaphore_signal(bar, inc=1, device_id=other, device_id_type=MESH)
        pl.semaphore_wait(bar, self.size + 1)


def remote(src, dst, send, recv, device):
    return pltpu.make_async_remote_copy(
        src_ref=src, dst_ref=dst, send_sem=send, recv_sem=recv, device_id=device, device_id_type=MESH
    )


def aligned(index, size):
    return pl.ds(pl.multiple_of(index * size, size), size)


def gather_kernel(planes, groups, q_ref, k_ref, v_ref, g_ref, qo_ref, go_ref, kv_ref,
                  local, a2a_send, a2a_recv, z_send, z_recv, sib_send, sib_recv):
    at = Where(planes, groups)
    rows = q_ref.shape[0]
    wide = q_ref.shape[1] // (NS * groups)
    half_rows = kv_ref.shape[2] // 2
    mine = aligned(at.p, rows)
    cols_own = aligned(at.g, HD)

    own_q = pltpu.make_async_copy(q_ref.at[:, aligned(at.g * NS + at.s, wide)], qo_ref.at[mine], local.at[0])
    own_g = pltpu.make_async_copy(g_ref.at[:, aligned(at.g * NS + at.s, wide)], go_ref.at[mine], local.at[1])
    own_k = pltpu.make_async_copy(k_ref.at[:, cols_own], kv_ref.at[0, at.z, mine], local.at[2])
    own_v = pltpu.make_async_copy(v_ref.at[:, cols_own], kv_ref.at[1, at.z, mine], local.at[2])
    own_q.start()
    own_g.start()

    @pl.when(at.core == 0)
    def _():
        own_k.start()

    @pl.when(at.core == 1)
    def _():
        own_v.start()

    at.greet()

    def send_kv(i, carry):
        _, os, og, device = at.peer(i)
        cols = aligned(og, HD)

        @pl.when(os % 2 == 0)
        def _():
            remote(k_ref.at[:, cols], kv_ref.at[0, at.z, mine], a2a_send.at[0], a2a_recv.at[0], device).start()

        @pl.when(os % 2 == 1)
        def _():
            remote(v_ref.at[:, cols], kv_ref.at[1, at.z, mine], a2a_send.at[0], a2a_recv.at[0], device).start()

        return carry

    lax.fori_loop(1, at.size, send_kv, 0)

    def send_q(i, carry):
        _, os, og, device = at.peer(i)
        cols = aligned(og * NS + os, wide)
        remote(q_ref.at[:, cols], qo_ref.at[mine], a2a_send.at[1], a2a_recv.at[1], device).start()
        remote(g_ref.at[:, cols], go_ref.at[mine], a2a_send.at[2], a2a_recv.at[2], device).start()
        return carry

    lax.fori_loop(1, at.size, send_q, 0)

    others = pl.ds(0, rows * (at.size - 1))
    own_k.wait()
    got = kv_ref.at[at.core, at.z, others]
    remote(got, got, a2a_send.at[0], a2a_recv.at[0], at.up).wait_recv()

    def piece(chunk, half):
        return kv_ref.at[at.core, chunk, pl.ds(half * half_rows, half_rows)]

    own = kv_ref.at[at.core, at.z]
    hops = planes // 2

    def moves(j, half, way):
        return j < hops - 1 or half == way

    def chunk_at(j, way):
        return (at.z + planes - j) % planes if way == 0 else (at.z + j) % planes

    def send(j, half, way):
        ref = piece(chunk_at(j, way), half)
        slot = (way, 2 * j + half)
        return remote(ref, ref, z_send.at[slot], z_recv.at[slot], at.up if way == 0 else at.down)

    def arrival(j, half, way):
        ref = piece(chunk_at(j + 1, way), half)
        slot = (way, 2 * j + half)
        return remote(ref, ref, z_send.at[slot], z_recv.at[slot], at.up if way == 0 else at.down)

    for j in range(hops):
        for half in (0, 1):
            for way in (0, 1):
                if j > 0:
                    arrival(j - 1, half, way).wait_recv()
                if moves(j, half, way):
                    send(j, half, way).start()
                if j > 0:
                    ref = piece(chunk_at(j, way), half)
                    remote(ref, ref, sib_send, sib_recv, at.sib).start()
        if j == 0:
            remote(own, own, sib_send, sib_recv, at.sib).start()
    for way in (0, 1):
        arrival(hops - 1, way, way).wait_recv()
        ref = piece(chunk_at(hops, way), way)
        remote(ref, ref, sib_send, sib_recv, at.sib).start()

    own_q.wait()
    own_g.wait()
    for n, (src, dst) in enumerate(((q_ref, qo_ref), (g_ref, go_ref))):
        sent = src.at[:, pl.ds(0, wide * (at.size - 1))]
        came = dst.at[others]
        remote(came, came, a2a_send.at[n + 1], a2a_recv.at[n + 1], at.up).wait_recv()
        remote(sent, sent, a2a_send.at[n + 1], a2a_recv.at[n + 1], at.up).wait_send()
    remote(got, got, a2a_send.at[0], a2a_recv.at[0], at.up).wait_send()
    for j in range(hops):
        for half in (0, 1):
            for way in (0, 1):
                if moves(j, half, way):
                    send(j, half, way).wait_send()
    sent = kv_ref.at[at.core]
    came = kv_ref.at[1 - at.core]
    remote(sent, sent, sib_send, sib_recv, at.sib).wait_send()
    remote(came, came, sib_send, sib_recv, at.sib).wait_recv()


def gather(planes, groups, queries, keys, values, out_grad):
    rows = queries.shape[0]
    plane_rows = rows * NS * groups
    wide = queries.shape[1] // (NS * groups)
    hops = planes // 2
    any_space = pl.BlockSpec(memory_space=pl.ANY)
    return pl.pallas_call(
        functools.partial(gather_kernel, planes, groups),
        out_shape=(
            jax.ShapeDtypeStruct((plane_rows, wide), BF16),
            jax.ShapeDtypeStruct((plane_rows, wide), BF16),
            jax.ShapeDtypeStruct((2, planes, plane_rows, HD), BF16),
        ),
        in_specs=[any_space] * 4,
        out_specs=(any_space,) * 3,
        scratch_shapes=[
            pltpu.SemaphoreType.DMA((3,)),
            pltpu.SemaphoreType.DMA((3,)),
            pltpu.SemaphoreType.DMA((3,)),
            pltpu.SemaphoreType.DMA((2, 2 * hops)),
            pltpu.SemaphoreType.DMA((2, 2 * hops)),
            pltpu.SemaphoreType.DMA,
            pltpu.SemaphoreType.DMA,
        ],
        compiler_params=pltpu.CompilerParams(collective_id=0, has_side_effects=True),
        name="gather",
    )(queries, keys, values, out_grad)


def attend_kernel(order_ref, doc_ref, plane_ref, q_ref, g_ref, doc2_ref, kv_ref, att_ref, dq_ref, dkv_ref,
                  k_s, v_s, kt_s, vt_s, dk_s, dv_s, s_s, p_s, acc_s, sem):
    tokens = kv_ref.shape[1]
    blocks = tokens // BLK
    own_blocks = q_ref.shape[0] // BLK
    heads = q_ref.shape[1] // HD
    rows = heads * BLK
    padded = k_s.shape[0]

    def fetch(i, carry):
        src, dst = aligned(i, BLK), aligned(order_ref[i], BLK)
        pltpu.make_async_copy(kv_ref.at[0, src], k_s.at[dst], sem.at[0]).start()
        pltpu.make_async_copy(kv_ref.at[1, src], v_s.at[dst], sem.at[1]).start()
        return carry

    lax.fori_loop(0, blocks, fetch, 0)
    tail = pl.ds(tokens, padded - tokens)
    k_s[tail, :] = jnp.zeros((padded - tokens, HD), BF16)
    v_s[tail, :] = jnp.zeros((padded - tokens, HD), BF16)
    kt_s[:, tail] = jnp.zeros((HD, padded - tokens), BF16)
    vt_s[:, tail] = jnp.zeros((HD, padded - tokens), BF16)

    def clear(i, carry):
        at = aligned(i, KTILE)
        dk_s[at, :] = jnp.zeros((KTILE, HD), F32)
        dv_s[at, :] = jnp.zeros((KTILE, HD), F32)
        return carry

    lax.fori_loop(0, padded // KTILE, clear, 0)
    whole = pl.ds(0, tokens)
    pltpu.make_async_copy(kv_ref.at[0], k_s.at[whole], sem.at[0]).wait()
    pltpu.make_async_copy(kv_ref.at[1], v_s.at[whole], sem.at[1]).wait()

    def eye(n):
        return (lax.broadcasted_iota(jnp.int32, (n, n), 0) == lax.broadcasted_iota(jnp.int32, (n, n), 1)).astype(
            F32).astype(BF16)

    eye_d = eye(HD)
    eye_r = eye(rows)

    def turn(i, carry):
        at = aligned(i, KTILE)
        kt_s[:, at] = dot(eye_d, k_s[at, :], NT).astype(BF16)
        vt_s[:, at] = dot(eye_d, v_s[at, :], NT).astype(BF16)
        return carry

    lax.fori_loop(0, tokens // KTILE, turn, 0)

    def query_block(n, carry):
        packed = order_ref[plane_ref[0] * own_blocks + n]
        first = packed * BLK
        doc0 = doc_ref[first]

        def halve(_, span):
            lo, hi = span
            mid = (lo + hi) // 2
            below = doc_ref[mid] < doc0
            return jnp.where(below, mid + 1, lo), jnp.where(below, hi, mid)

        doc_start, _ = lax.fori_loop(0, tokens.bit_length(), halve, (jnp.int32(0), first))
        base = (doc_start // BLK) * BLK
        tiles = (first + BLK - base + KTILE - 1) // KTILE

        lane = lax.broadcasted_iota(jnp.int32, (8, BLK), 1)
        docs = jnp.broadcast_to(doc2_ref[pl.ds(packed, 1), :], (8, BLK))
        opens = (lane > 0) & (docs != pltpu.roll(docs, 1, 1))
        begin = jnp.where(opens, first + lane, doc_start)
        step = 1
        while step < BLK:
            begin = jnp.maximum(begin, jnp.where(lane >= step, pltpu.roll(begin, step, 1), 0))
            step *= 2
        low = jnp.concatenate([begin[:1]] * heads, axis=1) - base
        high = jnp.concatenate([(first + lane)[:1]] * heads, axis=1) - base

        here = aligned(n, BLK)
        qs = jnp.concatenate([q_ref[here, h * HD:(h + 1) * HD] for h in range(heads)], axis=0)
        gs = jnp.concatenate([g_ref[here, h * HD:(h + 1) * HD] for h in range(heads)], axis=0)
        key_at = lax.broadcasted_iota(jnp.int32, (KTILE, rows), 0)

        def score_tile(t, top):
            at = pl.ds(pl.multiple_of(base + t * KTILE, BLK), KTILE)
            score = dot(k_s[at, :], qs, NT) * (SCALE * LOG2E)
            seen = (key_at >= low - t * KTILE) & (key_at <= high - t * KTILE)
            score = jnp.where(seen, score, NEG)
            s_s[aligned(t, KTILE), :] = score
            return jnp.maximum(top, jnp.max(score.reshape(KTILE // 8, 8, rows), axis=0))

        top = lax.fori_loop(0, tiles, score_tile, jnp.full((8, rows), NEG, F32))
        top = jnp.max(top, axis=0, keepdims=True)
        acc_s[...] = jnp.zeros_like(acc_s)

        def prob_tile(t, total):
            at = pl.ds(pl.multiple_of(base + t * KTILE, BLK), KTILE)
            prob = jnp.exp2(s_s[aligned(t, KTILE), :] - top)
            rounded = prob.astype(BF16)
            p_s[aligned(t, KTILE), :] = rounded
            acc_s[...] += dot(vt_s[:, at], rounded, NN)
            return total + jnp.sum(prob.reshape(KTILE // 8, 8, rows), axis=0)

        total = lax.fori_loop(0, tiles, prob_tile, jnp.zeros((8, rows), F32))
        inverse = 1.0 / jnp.sum(total, axis=0, keepdims=True)
        att_t = (acc_s[...] * inverse).astype(BF16)
        g_t = dot(eye_d, gs, NT)
        q_t = dot(eye_d, qs, NT)
        delta = jnp.sum(g_t * att_t.astype(F32), axis=0, keepdims=True)
        g_n = (g_t * inverse).astype(BF16)
        q_n = (q_t * (inverse * SCALE)).astype(BF16)
        att = dot(eye_r, att_t, NT).astype(BF16)
        for h in range(heads):
            att_ref[here, h * HD:(h + 1) * HD] = att[h * BLK:(h + 1) * BLK]
        acc_s[...] = jnp.zeros_like(acc_s)

        def grad_tile(t, carry):
            at = pl.ds(pl.multiple_of(base + t * KTILE, BLK), KTILE)
            prob = p_s[aligned(t, KTILE), :]
            dprob = dot(v_s[at, :], gs, NT)
            dscore = (prob.astype(F32) * (dprob - delta)).astype(BF16)
            dv_s[at, :] += dot(prob, g_n, NT)
            dk_s[at, :] += dot(dscore, q_n, NT)
            acc_s[...] += dot(kt_s[:, at], dscore, NN)
            return carry

        lax.fori_loop(0, tiles, grad_tile, 0)
        dq_t = (acc_s[...] * (inverse * SCALE)).astype(BF16)
        dq = dot(eye_r, dq_t, NT).astype(BF16)
        for h in range(heads):
            dq_ref[here, h * HD:(h + 1) * HD] = dq[h * BLK:(h + 1) * BLK]
        return carry

    lax.fori_loop(0, own_blocks, query_block, 0)

    def hand_out(i, carry):
        src, dst = aligned(order_ref[i], BLK), aligned(i, BLK)
        dkv_ref[0, dst, :] = dk_s[src, :].astype(BF16)
        dkv_ref[1, dst, :] = dv_s[src, :].astype(BF16)
        return carry

    lax.fori_loop(0, blocks, hand_out, 0)


def attend(plane, q_loc, g_loc, kv, doc_ids, block_order):
    tokens = kv.shape[1]
    wide = q_loc.shape[1]
    rows = wide // HD * BLK
    padded = tokens + KTILE
    longest = (min(tokens, 4096) + BLK + KTILE - 1) // KTILE * KTILE
    vmem = pl.BlockSpec(memory_space=pltpu.VMEM)
    smem = pl.BlockSpec(memory_space=pltpu.SMEM)
    return pl.pallas_call(
        attend_kernel,
        out_shape=(
            jax.ShapeDtypeStruct(q_loc.shape, BF16),
            jax.ShapeDtypeStruct(q_loc.shape, BF16),
            jax.ShapeDtypeStruct(kv.shape, BF16),
        ),
        in_specs=[smem, smem, smem, vmem, vmem, vmem, pl.BlockSpec(memory_space=pl.ANY)],
        out_specs=(vmem, vmem, vmem),
        scratch_shapes=[
            pltpu.VMEM((padded, HD), BF16),
            pltpu.VMEM((padded, HD), BF16),
            pltpu.VMEM((HD, padded), BF16),
            pltpu.VMEM((HD, padded), BF16),
            pltpu.VMEM((padded, HD), F32),
            pltpu.VMEM((padded, HD), F32),
            pltpu.VMEM((longest, rows), F32),
            pltpu.VMEM((longest, rows), BF16),
            pltpu.VMEM((HD, rows), F32),
            pltpu.SemaphoreType.DMA((2,)),
        ],
        compiler_params=pltpu.CompilerParams(vmem_limit_bytes=VMEM_LIMIT),
        name="attend",
    )(block_order, doc_ids, plane, q_loc, g_loc, doc_ids.reshape(tokens // BLK, BLK), kv)


def scatter_kernel(planes, groups, att_ref, dq_ref, dkv_ref, ao_ref, dqo_ref, kg_ref, vg_ref,
                   mine_s, sib_s, stage_s, came_s, fin_s, land_s,
                   local, mine_sem, sib_send, sib_recv, a2a_send, a2a_recv, z_send, z_recv):
    at = Where(planes, groups)
    rows = ao_ref.shape[0]
    wide = att_ref.shape[1]
    half_rows = dkv_ref.shape[2] // 2
    hops = planes // 2
    mine = aligned(at.p, rows)
    cols = aligned(at.g * NS + at.s, wide)

    own_a = pltpu.make_async_copy(att_ref.at[mine], ao_ref.at[:, cols], local.at[0])
    own_q = pltpu.make_async_copy(dq_ref.at[mine], dqo_ref.at[:, cols], local.at[1])
    own_a.start()
    own_q.start()

    turns = [hops]
    for j in range(hops - 1, 0, -1):
        turns += [j, -j]
    turns += [0]
    own_part, sib_part = [], []
    for n, distance in enumerate(turns):
        chunk = (at.z + planes + distance) % planes
        own_part.append(pltpu.make_async_copy(dkv_ref.at[at.core, chunk], mine_s.at[chunk], mine_sem.at[n]))
        sib_part.append(remote(dkv_ref.at[1 - at.core, chunk], sib_s.at[chunk],
                               sib_send.at[n], sib_recv.at[n], at.sib))
    for copy in own_part:
        copy.start()
    at.greet()
    for copy in sib_part:
        copy.start()

    def send_out(i, carry):
        o, _, _, device = at.peer(i)
        theirs = aligned(o, rows)
        remote(att_ref.at[theirs], ao_ref.at[:, cols], a2a_send.at[0], a2a_recv.at[0], device).start()
        remote(dq_ref.at[theirs], dqo_ref.at[:, cols], a2a_send.at[1], a2a_recv.at[1], device).start()
        return carry

    lax.fori_loop(1, at.size, send_out, 0)

    def ready(distance):
        n = turns.index(distance)
        own_part[n].wait()
        sib_part[n].wait_recv()

    def own_sum(distance, half):
        chunk = (at.z + planes + distance) % planes
        part = pl.ds(half * half_rows, half_rows)
        return mine_s[chunk, part, :].astype(F32) + sib_s[chunk, part, :].astype(F32)

    def moves(j, half, way):
        return j > 0 or half == way

    def send(j, half, way):
        slot = (way, 2 * j + half)
        return remote(stage_s.at[slot], came_s.at[slot], z_send.at[slot], z_recv.at[slot],
                      at.up if way == 0 else at.down)

    for j in range(hops):
        distance = hops - j
        if j == 0:
            ready(hops)
        else:
            ready(distance)
            ready(-distance)
        for turn in (0, 1):
            for way in (0, 1):
                half = 1 - way if turn == 0 else way
                if not moves(j, half, way):
                    continue
                value = own_sum(distance if way == 0 else -distance, half)
                if j > 0 and moves(j - 1, half, way):
                    send(j - 1, half, way).wait_recv()
                    value = value + came_s[way, 2 * (j - 1) + half].astype(F32)
                stage_s[way, 2 * j + half] = value.astype(BF16)
                send(j, half, way).start()

    ready(0)
    for half in (0, 1):
        value = own_sum(0, half)
        for way in (0, 1):
            if moves(hops - 1, half, way):
                send(hops - 1, half, way).wait_recv()
                value = value + came_s[way, 2 * (hops - 1) + half].astype(F32)
        fin_s[pl.ds(half * half_rows, half_rows), :] = value.astype(BF16)

    group_cols = aligned(at.g, HD)
    target = land_s.at[at.core, at.ylo, :, group_cols]
    own_fin = pltpu.make_async_copy(fin_s.at[mine], target, local.at[2])
    own_fin.start()

    def send_fin(i, carry):
        o, _, _, device = at.peer(i)
        remote(fin_s.at[aligned(o, rows)], target, a2a_send.at[2], a2a_recv.at[2], device).start()
        return carry

    lax.fori_loop(1, at.size, send_fin, 0)

    others = pl.ds(0, rows * (at.size - 1))
    some = pl.ds(0, wide * (at.size - 1))
    own_a.wait()
    own_q.wait()
    for n, (src, dst) in enumerate(((att_ref, ao_ref), (dq_ref, dqo_ref))):
        sent, came = src.at[others], dst.at[:, some]
        remote(came, came, a2a_send.at[n], a2a_recv.at[n], at.up).wait_recv()
        remote(sent, sent, a2a_send.at[n], a2a_recv.at[n], at.up).wait_send()
    for j in range(hops):
        for half in (0, 1):
            for way in (0, 1):
                if moves(j, half, way):
                    send(j, half, way).wait_send()
    for copy in sib_part:
        copy.wait_send()
    own_fin.wait()
    moved = fin_s.at[others]
    remote(moved, moved, a2a_send.at[2], a2a_recv.at[2], at.up).wait()
    kg_ref[...] = (land_s[0, 0].astype(F32) + land_s[0, 1].astype(F32)).astype(BF16)
    vg_ref[...] = (land_s[1, 0].astype(F32) + land_s[1, 1].astype(F32)).astype(BF16)


def scatter(planes, groups, att, dq, dkv):
    plane_rows = att.shape[0]
    rows = plane_rows // (NS * groups)
    columns = att.shape[1] * NS * groups
    hops = planes // 2
    any_space = pl.BlockSpec(memory_space=pl.ANY)
    vmem = pl.BlockSpec(memory_space=pltpu.VMEM)
    dma = pltpu.SemaphoreType.DMA
    return pl.pallas_call(
        functools.partial(scatter_kernel, planes, groups),
        out_shape=(
            jax.ShapeDtypeStruct((rows, columns), BF16),
            jax.ShapeDtypeStruct((rows, columns), BF16),
            jax.ShapeDtypeStruct((rows, groups * HD), BF16),
            jax.ShapeDtypeStruct((rows, groups * HD), BF16),
        ),
        in_specs=[any_space] * 3,
        out_specs=(any_space, any_space, vmem, vmem),
        scratch_shapes=[
            pltpu.VMEM((planes, plane_rows, HD), BF16),
            pltpu.VMEM((planes, plane_rows, HD), BF16),
            pltpu.VMEM((2, 2 * hops, plane_rows // 2, HD), BF16),
            pltpu.VMEM((2, 2 * hops, plane_rows // 2, HD), BF16),
            pltpu.VMEM((plane_rows, HD), BF16),
            pltpu.VMEM((2, NS // 2, rows, groups * HD), BF16),
            dma((3,)),
            dma((planes,)),
            dma((planes,)),
            dma((planes,)),
            dma((3,)),
            dma((3,)),
            dma((2, 2 * hops)),
            dma((2, 2 * hops)),
        ],
        compiler_params=pltpu.CompilerParams(
            collective_id=1, has_side_effects=True, vmem_limit_bytes=VMEM_LIMIT
        ),
        name="scatter",
    )(att, dq, dkv)


def per_device(planes, groups, queries, keys, values, out_grad, doc_ids, block_order):
    plane = (lax.axis_index("ctx") // NS).astype(jnp.int32).reshape(1)
    q_loc, g_loc, kv = gather(planes, groups, queries, keys, values, out_grad)
    tokens = doc_ids.shape[0]
    att, dq, dkv = attend(plane, q_loc, g_loc, kv.reshape(2, tokens, HD), doc_ids, block_order)
    return scatter(planes, groups, att, dq, dkv.reshape(kv.shape))


def solution(mesh):
    split = P(("ctx", "head"), None)
    planes, groups = mesh.shape["ctx"] // NS, mesh.shape["head"]
    return jax.shard_map(
        functools.partial(per_device, planes, groups),
        mesh=mesh,
        in_specs=(split, split, split, split, P(), P()),
        out_specs=(split, split, split, split),
        check_vma=False,
    )
```

```python
import functools
import math

import jax
import jax.numpy as jnp
from jax import lax
from jax.experimental import pallas as pl
from jax.experimental.pallas import tpu as pltpu
from jax.sharding import PartitionSpec as P

QH = 64
KVH = 8
HD = 128
BLK = 128
NS = 4
KTILE = 2048
PAIR = 2 * BLK
LANES = 64
OUT = 4
FRONT = BLK
LOG2E = math.log2(math.e)
SCALE = 1.0 / math.sqrt(HD)
NEG = -1e30
MESH = pl.DeviceIdType.MESH
F32 = jnp.float32
BF16 = jnp.bfloat16
NT = (((1,), (1,)), ((), ()))
NN = (((1,), (0,)), ((), ()))
VMEM_LIMIT = 56 * 1024 * 1024


def dot(a, b, dims):
    return lax.dot_general(a, b, dims, preferred_element_type=F32)


class Where:
    def __init__(self, planes, groups):
        ctx = lax.axis_index("ctx")
        self.planes, self.groups = planes, groups
        self.size = NS * groups
        self.g = lax.axis_index("head")
        self.z, self.s = ctx // NS, ctx % NS
        self.core, self.ylo = self.s % 2, self.s // 2
        self.p = self.s * groups + self.g
        self.up = (((self.z + 1) % planes) * NS + self.s, self.g)
        self.down = (((self.z + planes - 1) % planes) * NS + self.s, self.g)
        self.sib = (ctx + 1 - 2 * self.core, self.g)

    def peer(self, i):
        o = (self.p + i) % self.size
        return o, o // self.groups, o % self.groups, (self.z * NS + o // self.groups, o % self.groups)

    def greet(self):
        bar = pltpu.get_barrier_semaphore()

        def signal(i, carry):
            pl.semaphore_signal(bar, inc=1, device_id=self.peer(i)[3], device_id_type=MESH)
            return carry

        lax.fori_loop(1, self.size, signal, 0)
        for other in (self.up, self.down):
            pl.semaphore_signal(bar, inc=1, device_id=other, device_id_type=MESH)
        pl.semaphore_wait(bar, self.size + 1)


def remote(src, dst, send, recv, device):
    return pltpu.make_async_remote_copy(
        src_ref=src, dst_ref=dst, send_sem=send, recv_sem=recv, device_id=device, device_id_type=MESH
    )


def aligned(index, size):
    return pl.ds(pl.multiple_of(index * size, size), size)


def gather_kernel(planes, groups, q_ref, k_ref, v_ref, g_ref, qo_ref, go_ref, kv_ref,
                  local, a2a_send, a2a_recv, z_send, z_recv, sib_send, sib_recv):
    at = Where(planes, groups)
    rows = q_ref.shape[0]
    wide = q_ref.shape[1] // (NS * groups)
    half_rows = kv_ref.shape[2] // 2
    mine = aligned(at.p, rows)
    cols_own = aligned(at.g, HD)

    own_q = pltpu.make_async_copy(q_ref.at[:, aligned(at.g * NS + at.s, wide)], qo_ref.at[mine], local.at[0])
    own_g = pltpu.make_async_copy(g_ref.at[:, aligned(at.g * NS + at.s, wide)], go_ref.at[mine], local.at[1])
    own_k = pltpu.make_async_copy(k_ref.at[:, cols_own], kv_ref.at[0, at.z, mine], local.at[2])
    own_v = pltpu.make_async_copy(v_ref.at[:, cols_own], kv_ref.at[1, at.z, mine], local.at[2])
    own_q.start()
    own_g.start()

    @pl.when(at.core == 0)
    def _():
        own_k.start()

    @pl.when(at.core == 1)
    def _():
        own_v.start()

    at.greet()

    def send_kv(i, carry):
        _, os, og, device = at.peer(i)
        cols = aligned(og, HD)

        @pl.when(os % 2 == 0)
        def _():
            remote(k_ref.at[:, cols], kv_ref.at[0, at.z, mine], a2a_send.at[0], a2a_recv.at[0], device).start()

        @pl.when(os % 2 == 1)
        def _():
            remote(v_ref.at[:, cols], kv_ref.at[1, at.z, mine], a2a_send.at[0], a2a_recv.at[0], device).start()

        return carry

    lax.fori_loop(1, at.size, send_kv, 0)

    def send_q(i, carry):
        _, os, og, device = at.peer(i)
        cols = aligned(og * NS + os, wide)
        remote(q_ref.at[:, cols], qo_ref.at[mine], a2a_send.at[1], a2a_recv.at[1], device).start()
        remote(g_ref.at[:, cols], go_ref.at[mine], a2a_send.at[2], a2a_recv.at[2], device).start()
        return carry

    lax.fori_loop(1, at.size, send_q, 0)

    others = pl.ds(0, rows * (at.size - 1))
    own_k.wait()
    got = kv_ref.at[at.core, at.z, others]
    remote(got, got, a2a_send.at[0], a2a_recv.at[0], at.up).wait_recv()

    def piece(chunk, half):
        return kv_ref.at[at.core, chunk, pl.ds(half * half_rows, half_rows)]

    own = kv_ref.at[at.core, at.z]
    hops = planes // 2

    def moves(j, half, way):
        return j < hops - 1 or half == way

    def chunk_at(j, way):
        return (at.z + planes - j) % planes if way == 0 else (at.z + j) % planes

    def send(j, half, way):
        ref = piece(chunk_at(j, way), half)
        slot = (way, 2 * j + half)
        return remote(ref, ref, z_send.at[slot], z_recv.at[slot], at.up if way == 0 else at.down)

    def arrival(j, half, way):
        ref = piece(chunk_at(j + 1, way), half)
        slot = (way, 2 * j + half)
        return remote(ref, ref, z_send.at[slot], z_recv.at[slot], at.up if way == 0 else at.down)

    for j in range(hops):
        for half in (0, 1):
            for way in (0, 1):
                if j > 0:
                    arrival(j - 1, half, way).wait_recv()
                if moves(j, half, way):
                    send(j, half, way).start()
                if j > 0:
                    ref = piece(chunk_at(j, way), half)
                    remote(ref, ref, sib_send, sib_recv, at.sib).start()
        if j == 0:
            remote(own, own, sib_send, sib_recv, at.sib).start()
    for way in (0, 1):
        arrival(hops - 1, way, way).wait_recv()
        ref = piece(chunk_at(hops, way), way)
        remote(ref, ref, sib_send, sib_recv, at.sib).start()

    own_q.wait()
    own_g.wait()
    for n, (src, dst) in enumerate(((q_ref, qo_ref), (g_ref, go_ref))):
        sent = src.at[:, pl.ds(0, wide * (at.size - 1))]
        came = dst.at[others]
        remote(came, came, a2a_send.at[n + 1], a2a_recv.at[n + 1], at.up).wait_recv()
        remote(sent, sent, a2a_send.at[n + 1], a2a_recv.at[n + 1], at.up).wait_send()
    remote(got, got, a2a_send.at[0], a2a_recv.at[0], at.up).wait_send()
    for j in range(hops):
        for half in (0, 1):
            for way in (0, 1):
                if moves(j, half, way):
                    send(j, half, way).wait_send()
    sent = kv_ref.at[at.core]
    came = kv_ref.at[1 - at.core]
    remote(sent, sent, sib_send, sib_recv, at.sib).wait_send()
    remote(came, came, sib_send, sib_recv, at.sib).wait_recv()


def gather(planes, groups, queries, keys, values, out_grad):
    rows = queries.shape[0]
    plane_rows = rows * NS * groups
    wide = queries.shape[1] // (NS * groups)
    hops = planes // 2
    any_space = pl.BlockSpec(memory_space=pl.ANY)
    return pl.pallas_call(
        functools.partial(gather_kernel, planes, groups),
        out_shape=(
            jax.ShapeDtypeStruct((plane_rows, wide), BF16),
            jax.ShapeDtypeStruct((plane_rows, wide), BF16),
            jax.ShapeDtypeStruct((2, planes, plane_rows, HD), BF16),
        ),
        in_specs=[any_space] * 4,
        out_specs=(any_space,) * 3,
        scratch_shapes=[
            pltpu.SemaphoreType.DMA((3,)),
            pltpu.SemaphoreType.DMA((3,)),
            pltpu.SemaphoreType.DMA((3,)),
            pltpu.SemaphoreType.DMA((2, 2 * hops)),
            pltpu.SemaphoreType.DMA((2, 2 * hops)),
            pltpu.SemaphoreType.DMA,
            pltpu.SemaphoreType.DMA,
        ],
        compiler_params=pltpu.CompilerParams(
            collective_id=0, has_side_effects=True, vmem_limit_bytes=VMEM_LIMIT
        ),
        name="gather",
    )(queries, keys, values, out_grad)


def attend_kernel(order_ref, doc_ref, plane_ref, doc2_ref, q_ref, g_ref, kv_ref, att_ref, dq_ref, dkv_ref,
                  q_s, g_s, att_s, dq_s, kv_s, kvt_s, dkv_s, out_s, s_s, p_s, acc_s, top_s, total_s,
                  begin_s, start_s, sem):
    tokens = kv_ref.shape[1]
    blocks = tokens // BLK
    own_blocks = q_ref.shape[0] // BLK
    heads = q_ref.shape[1] // HD
    rows = heads * BLK
    turned = min(tokens, 2048)

    def fetch(i, carry):
        dst = pl.ds(pl.multiple_of(FRONT + order_ref[i] * BLK, BLK), BLK)
        pltpu.make_async_copy(kv_ref.at[:, aligned(i, BLK)], kv_s.at[:, dst], sem.at[0]).start()
        return carry

    lax.fori_loop(0, blocks, fetch, 0)
    load_q = pltpu.make_async_copy(q_ref, q_s, sem.at[2])
    load_g = pltpu.make_async_copy(g_ref, g_s, sem.at[3])
    load_q.start()
    load_g.start()
    head = pl.ds(0, FRONT)
    kv_s[:, head, :] = jnp.zeros((2, FRONT, HD), BF16)
    kvt_s[:, :, head] = jnp.zeros((2, HD, FRONT), BF16)
    dkv_s[:, head, :] = jnp.zeros((2, FRONT, HD), F32)

    def clear(i, carry):
        at = pl.ds(pl.multiple_of(FRONT + i * 512, BLK), 512)
        dkv_s[:, at, :] = jnp.zeros((2, 512, HD), F32)
        return carry

    lax.fori_loop(0, tokens // 512, clear, 0)

    def eye(n):
        return (lax.broadcasted_iota(jnp.int32, (n, n), 0) == lax.broadcasted_iota(jnp.int32, (n, n), 1)).astype(
            F32).astype(BF16)

    eye_d = eye(HD)
    eye_r = eye(rows)
    packed = [order_ref[plane_ref[0] * own_blocks + n] for n in range(own_blocks)]
    firsts = [b * BLK for b in packed]
    wanted = [doc_ref[first] for first in firsts]

    def halve(_, spans):
        lows, highs = [], []
        for (lo, hi), doc0 in zip(spans, wanted):
            mid = (lo + hi) // 2
            below = doc_ref[mid] < doc0
            lows.append(jnp.where(below, mid + 1, lo))
            highs.append(jnp.where(below, hi, mid))
        return tuple(zip(lows, highs))

    spans = lax.fori_loop(0, tokens.bit_length(), halve, tuple((jnp.int32(0), first) for first in firsts))
    starts = [lo for lo, _ in spans]
    for n in range(own_blocks):
        start_s[n] = starts[n]
    lane = lax.broadcasted_iota(jnp.int32, (own_blocks, BLK), 1)
    docs = jnp.concatenate([doc2_ref[pl.ds(b, 1), :] for b in packed], axis=0)
    opens = (lane > 0) & (docs != pltpu.roll(docs, 1, 1))
    first_of = jnp.concatenate([jnp.full((1, BLK), first, jnp.int32) for first in firsts], axis=0)
    start_of = jnp.concatenate([jnp.full((1, BLK), start, jnp.int32) for start in starts], axis=0)
    begin = jnp.where(opens, first_of + lane, start_of)
    step = 1
    while step < BLK:
        begin = jnp.maximum(begin, jnp.where(lane >= step, pltpu.roll(begin, step, 1), 0))
        step *= 2
    begin_s[...] = begin
    pltpu.make_async_copy(kv_ref, kv_s.at[:, pl.ds(FRONT, tokens)], sem.at[0]).wait()

    def turn(i, carry):
        at = pl.ds(pl.multiple_of(FRONT + i * turned, BLK), turned)
        kvt_s[0, :, at] = dot(eye_d, kv_s[0, at, :], NT).astype(BF16)
        kvt_s[1, :, at] = dot(eye_d, kv_s[1, at, :], NT).astype(BF16)
        return carry

    lax.fori_loop(0, tokens // turned, turn, 0)

    def query_block(n, carry):
        packed = order_ref[plane_ref[0] * own_blocks + n]
        first = packed * BLK
        doc_start = start_s[n]
        pairs = (first // BLK - doc_start // BLK + PAIR // BLK) // (PAIR // BLK)
        base = FRONT + first + BLK - pairs * PAIR
        lead = (pairs - 1) % (KTILE // PAIR) + 1
        tiles = (pairs - 1) // (KTILE // PAIR)

        def each_tile(work):
            for size in range(1, KTILE // PAIR + 1):
                @pl.when(lead == size)
                def _():
                    work(0, size * PAIR, True)

            def step(t, carry):
                work(pl.multiple_of(lead * PAIR + t * KTILE, PAIR), KTILE, False)
                return carry

            lax.fori_loop(0, tiles, step, 0)

        begin = begin_s[pl.ds(n, 1), :]
        lane = lax.broadcasted_iota(jnp.int32, (1, BLK), 1)
        bias = jnp.where(begin > doc_start, NEG, 0.0)
        bias = jnp.concatenate([bias] * heads, axis=1)
        low = jnp.concatenate([begin] * heads, axis=1) + (FRONT - base)
        high = jnp.concatenate([first + lane] * heads, axis=1) + (FRONT - base)

        here = aligned(n, BLK)
        qs = jnp.concatenate([q_s[here, h * HD:(h + 1) * HD] for h in range(heads)], axis=0)
        gs = jnp.concatenate([g_s[here, h * HD:(h + 1) * HD] for h in range(heads)], axis=0)

        def score_tile(rel, width, leads):
            score = dot(kv_s[0, pl.ds(pl.multiple_of(base + rel, BLK), width), :], qs, NT)
            cuts = [(0, PAIR, True)] if leads else []
            if leads and width > PAIR:
                cuts += [(PAIR, width - BLK, False), (width - BLK, width, True)]
            elif not leads:
                cuts = [(0, width - BLK, False), (width - BLK, width, True)]
            top = None
            for start, end, edge in cuts:
                count = end - start
                part = score[start:end] * (SCALE * LOG2E)
                if edge:
                    key_at = lax.broadcasted_iota(jnp.int32, (count, rows), 0)
                    seen = (key_at >= low - (rel + start)) & (key_at <= high - (rel + start))
                    part = jnp.where(seen, part, NEG)
                else:
                    part = part + bias
                s_s[pl.ds(pl.multiple_of(rel + start, BLK), count), :] = part
                most = jnp.max(part.reshape(count // LANES, LANES, rows), axis=0)
                top = most if top is None else jnp.maximum(top, most)
            top_s[...] = top if leads else jnp.maximum(top_s[...], top)

        each_tile(score_tile)
        top = jnp.max(top_s[...], axis=0, keepdims=True)

        def prob_tile(rel, width, leads):
            at = pl.ds(pl.multiple_of(base + rel, BLK), width)
            there = pl.ds(pl.multiple_of(rel, PAIR), width)
            prob = jnp.exp2(s_s[there, :] - top)
            rounded = prob.astype(BF16)
            p_s[there, :] = rounded
            part = dot(kvt_s[1, :, at], rounded, NN)
            total = jnp.sum(prob.reshape(width // LANES, LANES, rows), axis=0)
            if leads:
                acc_s[...] = part
                total_s[...] = total
            else:
                acc_s[...] += part
                total_s[...] += total

        each_tile(prob_tile)
        inverse = 1.0 / jnp.sum(total_s[...], axis=0, keepdims=True)
        att_t = (acc_s[...] * inverse).astype(BF16)
        g_t = dot(eye_d, gs, NT)
        q_t = dot(eye_d, qs, NT)
        delta = jnp.sum(g_t * att_t.astype(F32), axis=0, keepdims=True)
        g_n = (g_t * inverse).astype(BF16)
        q_n = (q_t * (inverse * SCALE)).astype(BF16)
        att = dot(eye_r, att_t, NT).astype(BF16)
        for h in range(heads):
            att_s[here, h * HD:(h + 1) * HD] = att[h * BLK:(h + 1) * BLK]

        def grad_tile(rel, width, leads):
            at = pl.ds(pl.multiple_of(base + rel, BLK), width)
            prob = p_s[pl.ds(pl.multiple_of(rel, PAIR), width), :]
            dprob = dot(kv_s[1, at, :], gs, NT)
            dscore = (prob.astype(F32) * (dprob - delta)).astype(BF16)
            dkv_s[1, at, :] += dot(prob, g_n, NT)
            dkv_s[0, at, :] += dot(dscore, q_n, NT)
            part = dot(kvt_s[0, :, at], dscore, NN)
            if leads:
                acc_s[...] = part
            else:
                acc_s[...] += part

        each_tile(grad_tile)
        dq_t = (acc_s[...] * (inverse * SCALE)).astype(BF16)
        dq = dot(eye_r, dq_t, NT).astype(BF16)
        for h in range(heads):
            dq_s[here, h * HD:(h + 1) * HD] = dq[h * BLK:(h + 1) * BLK]
        pltpu.make_async_copy(att_s.at[here], att_ref.at[here], sem.at[2]).start()
        pltpu.make_async_copy(dq_s.at[here], dq_ref.at[here], sem.at[3]).start()
        return carry

    load_q.wait()
    load_g.wait()
    lax.fori_loop(0, own_blocks, query_block, 0)

    def hand_out(i, carry):
        for j in range(OUT):
            src = pl.ds(pl.multiple_of(FRONT + order_ref[i * OUT + j] * BLK, BLK), BLK)
            dst = aligned(i * OUT + j, BLK)
            out_s[:, dst, :] = dkv_s[:, src, :].astype(BF16)
        dst = aligned(i, OUT * BLK)
        pltpu.make_async_copy(out_s.at[:, dst], dkv_ref.at[:, dst], sem.at[1]).start()
        return carry

    lax.fori_loop(0, blocks // OUT, hand_out, 0)
    pltpu.make_async_copy(att_s, att_ref, sem.at[2]).wait()
    pltpu.make_async_copy(dq_s, dq_ref, sem.at[3]).wait()
    pltpu.make_async_copy(out_s, dkv_ref, sem.at[1]).wait()


def attend(plane, q_loc, g_loc, kv, doc_ids, block_order):
    tokens = kv.shape[1]
    rows = q_loc.shape[1] // HD * BLK
    padded = FRONT + tokens
    longest = (min(tokens, 4096) + BLK + PAIR - 1) // PAIR * PAIR
    vmem = pl.BlockSpec(memory_space=pltpu.VMEM)
    smem = pl.BlockSpec(memory_space=pltpu.SMEM)
    any_space = pl.BlockSpec(memory_space=pl.ANY)
    return pl.pallas_call(
        attend_kernel,
        out_shape=(
            jax.ShapeDtypeStruct(q_loc.shape, BF16),
            jax.ShapeDtypeStruct(q_loc.shape, BF16),
            jax.ShapeDtypeStruct(kv.shape, BF16),
        ),
        in_specs=[smem, smem, smem, vmem, any_space, any_space, any_space],
        out_specs=(any_space,) * 3,
        scratch_shapes=[
            pltpu.VMEM(q_loc.shape, BF16),
            pltpu.VMEM(q_loc.shape, BF16),
            pltpu.VMEM(q_loc.shape, BF16),
            pltpu.VMEM(q_loc.shape, BF16),
            pltpu.VMEM((2, padded, HD), BF16),
            pltpu.VMEM((2, HD, padded), BF16),
            pltpu.VMEM((2, padded, HD), F32),
            pltpu.VMEM((2, tokens, HD), BF16),
            pltpu.VMEM((longest, rows), F32),
            pltpu.VMEM((longest, rows), BF16),
            pltpu.VMEM((HD, rows), F32),
            pltpu.VMEM((LANES, rows), F32),
            pltpu.VMEM((LANES, rows), F32),
            pltpu.VMEM((q_loc.shape[0] // BLK, BLK), jnp.int32),
            pltpu.SMEM((q_loc.shape[0] // BLK,), jnp.int32),
            pltpu.SemaphoreType.DMA((4,)),
        ],
        compiler_params=pltpu.CompilerParams(vmem_limit_bytes=VMEM_LIMIT),
        name="attend",
    )(block_order, doc_ids, plane, doc_ids.reshape(tokens // BLK, BLK), q_loc, g_loc, kv)


def scatter_kernel(planes, groups, att_ref, dq_ref, dkv_ref, ao_ref, dqo_ref, land_s,
                   mine_s, sib_s, stage_s, came_s, fin_s,
                   local, mine_sem, sib_send, sib_recv, a2a_send, a2a_recv, z_send, z_recv):
    at = Where(planes, groups)
    rows = ao_ref.shape[0]
    wide = att_ref.shape[1]
    half_rows = dkv_ref.shape[2] // 2
    hops = planes // 2
    mine = aligned(at.p, rows)
    cols = aligned(at.g * NS + at.s, wide)

    own_a = pltpu.make_async_copy(att_ref.at[mine], ao_ref.at[:, cols], local.at[0])
    own_q = pltpu.make_async_copy(dq_ref.at[mine], dqo_ref.at[:, cols], local.at[1])
    own_a.start()
    own_q.start()

    turns = [hops]
    for j in range(hops - 1, 0, -1):
        turns += [j, -j]
    turns += [0]
    own_part, sib_part = [], []
    for n, distance in enumerate(turns):
        chunk = (at.z + planes + distance) % planes
        own_part.append(pltpu.make_async_copy(dkv_ref.at[at.core, chunk], mine_s.at[chunk], mine_sem.at[n]))
        sib_part.append(remote(dkv_ref.at[1 - at.core, chunk], sib_s.at[chunk],
                               sib_send.at[n], sib_recv.at[n], at.sib))
    for copy in own_part:
        copy.start()
    at.greet()
    for copy in sib_part:
        copy.start()

    def send_out(i, carry):
        o, _, _, device = at.peer(i)
        theirs = aligned(o, rows)
        remote(att_ref.at[theirs], ao_ref.at[:, cols], a2a_send.at[0], a2a_recv.at[0], device).start()
        remote(dq_ref.at[theirs], dqo_ref.at[:, cols], a2a_send.at[1], a2a_recv.at[1], device).start()
        return carry

    lax.fori_loop(1, at.size, send_out, 0)

    def ready(distance):
        n = turns.index(distance)
        own_part[n].wait()
        sib_part[n].wait_recv()

    def own_sum(distance, half):
        chunk = (at.z + planes + distance) % planes
        part = pl.ds(half * half_rows, half_rows)
        return mine_s[chunk, part, :].astype(F32) + sib_s[chunk, part, :].astype(F32)

    def moves(j, half, way):
        return j > 0 or half == way

    def send(j, half, way):
        slot = (way, 2 * j + half)
        return remote(stage_s.at[slot], came_s.at[slot], z_send.at[slot], z_recv.at[slot],
                      at.up if way == 0 else at.down)

    for j in range(hops):
        distance = hops - j
        if j == 0:
            ready(hops)
        else:
            ready(distance)
            ready(-distance)
        for turn in (0, 1):
            for way in (0, 1):
                half = 1 - way if turn == 0 else way
                if not moves(j, half, way):
                    continue
                value = own_sum(distance if way == 0 else -distance, half)
                if j > 0 and moves(j - 1, half, way):
                    send(j - 1, half, way).wait_recv()
                    value = value + came_s[way, 2 * (j - 1) + half].astype(F32)
                stage_s[way, 2 * j + half] = value.astype(BF16)
                send(j, half, way).start()

    ready(0)
    for half in (0, 1):
        value = own_sum(0, half)
        for way in (0, 1):
            if moves(hops - 1, half, way):
                send(hops - 1, half, way).wait_recv()
                value = value + came_s[way, 2 * (hops - 1) + half].astype(F32)
        fin_s[pl.ds(half * half_rows, half_rows), :] = value.astype(BF16)

    group_cols = aligned(at.g, HD)
    target = land_s.at[at.core, at.ylo, :, group_cols]
    own_fin = pltpu.make_async_copy(fin_s.at[mine], target, local.at[2])
    own_fin.start()

    def send_fin(i, carry):
        o, _, _, device = at.peer(i)
        remote(fin_s.at[aligned(o, rows)], target, a2a_send.at[2], a2a_recv.at[2], device).start()
        return carry

    lax.fori_loop(1, at.size, send_fin, 0)

    others = pl.ds(0, rows * (at.size - 1))
    some = pl.ds(0, wide * (at.size - 1))
    own_a.wait()
    own_q.wait()
    for n, (src, dst) in enumerate(((att_ref, ao_ref), (dq_ref, dqo_ref))):
        sent, came = src.at[others], dst.at[:, some]
        remote(came, came, a2a_send.at[n], a2a_recv.at[n], at.up).wait_recv()
        remote(sent, sent, a2a_send.at[n], a2a_recv.at[n], at.up).wait_send()
    for j in range(hops):
        for half in (0, 1):
            for way in (0, 1):
                if moves(j, half, way):
                    send(j, half, way).wait_send()
    for copy in sib_part:
        copy.wait_send()
    own_fin.wait()
    moved = fin_s.at[others]
    remote(moved, moved, a2a_send.at[2], a2a_recv.at[2], at.up).wait()


def scatter(planes, groups, att, dq, dkv):
    plane_rows = att.shape[0]
    rows = plane_rows // (NS * groups)
    columns = att.shape[1] * NS * groups
    hops = planes // 2
    any_space = pl.BlockSpec(memory_space=pl.ANY)
    dma = pltpu.SemaphoreType.DMA
    return pl.pallas_call(
        functools.partial(scatter_kernel, planes, groups),
        out_shape=(
            jax.ShapeDtypeStruct((rows, columns), BF16),
            jax.ShapeDtypeStruct((rows, columns), BF16),
            jax.ShapeDtypeStruct((2, NS // 2, rows, groups * HD), BF16),
        ),
        in_specs=[any_space] * 3,
        out_specs=(any_space,) * 3,
        scratch_shapes=[
            pltpu.VMEM((planes, plane_rows, HD), BF16),
            pltpu.VMEM((planes, plane_rows, HD), BF16),
            pltpu.VMEM((2, 2 * hops, plane_rows // 2, HD), BF16),
            pltpu.VMEM((2, 2 * hops, plane_rows // 2, HD), BF16),
            pltpu.VMEM((plane_rows, HD), BF16),
            dma((3,)),
            dma((planes,)),
            dma((planes,)),
            dma((planes,)),
            dma((3,)),
            dma((3,)),
            dma((2, 2 * hops)),
            dma((2, 2 * hops)),
        ],
        compiler_params=pltpu.CompilerParams(
            collective_id=1, has_side_effects=True, vmem_limit_bytes=VMEM_LIMIT
        ),
        name="scatter",
    )(att, dq, dkv)


def finish_kernel(a_ref, q_ref, land_ref, ao_ref, qo_ref, kg_ref, vg_ref, sem):
    moves = [pltpu.make_async_copy(a_ref, ao_ref, sem.at[0]), pltpu.make_async_copy(q_ref, qo_ref, sem.at[1])]
    for move in moves:
        move.start()
    for part, out in ((0, kg_ref), (1, vg_ref)):
        total = land_ref[part, 0].astype(F32)
        for ylo in range(1, NS // 2):
            total = total + land_ref[part, ylo].astype(F32)
        out[...] = total.astype(BF16)
    for move in moves:
        move.wait()


def finish(att, dq, land):
    any_space = pl.BlockSpec(memory_space=pl.ANY)
    vmem = pl.BlockSpec(memory_space=pltpu.VMEM)
    grad = jax.ShapeDtypeStruct(land.shape[2:], BF16)
    return pl.pallas_call(
        finish_kernel,
        out_shape=(jax.ShapeDtypeStruct(att.shape, BF16), jax.ShapeDtypeStruct(dq.shape, BF16), grad, grad),
        in_specs=[any_space, any_space, vmem],
        out_specs=(any_space, any_space, vmem, vmem),
        scratch_shapes=[pltpu.SemaphoreType.DMA((2,))],
        name="finish",
    )(att, dq, land)


def per_device(planes, groups, queries, keys, values, out_grad, doc_ids, block_order):
    plane = (lax.axis_index("ctx") // NS).astype(jnp.int32).reshape(1)
    q_loc, g_loc, kv = gather(planes, groups, queries, keys, values, out_grad)
    tokens = doc_ids.shape[0]
    att, dq, dkv = attend(plane, q_loc, g_loc, kv.reshape(2, tokens, HD), doc_ids, block_order)
    return finish(*scatter(planes, groups, att, dq, dkv.reshape(kv.shape)))


def solution(mesh):
    split = P(("ctx", "head"), None)
    planes, groups = mesh.shape["ctx"] // NS, mesh.shape["head"]
    return jax.shard_map(
        functools.partial(per_device, planes, groups),
        mesh=mesh,
        in_specs=(split, split, split, split, P(), P()),
        out_specs=(split, split, split, split),
        check_vma=False,
    )
```

```python
import functools
import math

import jax
import jax.numpy as jnp
from jax import lax
from jax.experimental import pallas as pl
from jax.experimental.pallas import tpu as pltpu
from jax.sharding import PartitionSpec as P

QH = 64
KVH = 8
HD = 128
BLK = 128
NS = 4
KTILE = 2048
PAIR = 2 * BLK
LANES = 64
OUT = 4
FRONT = BLK
LOG2E = math.log2(math.e)
SCALE = 1.0 / math.sqrt(HD)
NEG = -1e30
MESH = pl.DeviceIdType.MESH
F32 = jnp.float32
BF16 = jnp.bfloat16
NT = (((1,), (1,)), ((), ()))
NN = (((1,), (0,)), ((), ()))
VMEM_LIMIT = 56 * 1024 * 1024


def dot(a, b, dims):
    return lax.dot_general(a, b, dims, preferred_element_type=F32)


class Where:
    def __init__(self, planes, groups):
        ctx = lax.axis_index("ctx")
        self.planes, self.groups = planes, groups
        self.size = NS * groups
        self.g = lax.axis_index("head")
        self.z, self.s = ctx // NS, ctx % NS
        self.core, self.ylo = self.s % 2, self.s // 2
        self.p = self.s * groups + self.g
        self.up = (((self.z + 1) % planes) * NS + self.s, self.g)
        self.down = (((self.z + planes - 1) % planes) * NS + self.s, self.g)
        self.sib = (ctx + 1 - 2 * self.core, self.g)

    def peer(self, i):
        o = (self.p + i) % self.size
        return o, o // self.groups, o % self.groups, (self.z * NS + o // self.groups, o % self.groups)

    def greet(self):
        bar = pltpu.get_barrier_semaphore()

        def signal(i, carry):
            pl.semaphore_signal(bar, inc=1, device_id=self.peer(i)[3], device_id_type=MESH)
            return carry

        lax.fori_loop(1, self.size, signal, 0)
        for other in (self.up, self.down):
            pl.semaphore_signal(bar, inc=1, device_id=other, device_id_type=MESH)
        pl.semaphore_wait(bar, self.size + 1)


def remote(src, dst, send, recv, device):
    return pltpu.make_async_remote_copy(
        src_ref=src, dst_ref=dst, send_sem=send, recv_sem=recv, device_id=device, device_id_type=MESH
    )


def aligned(index, size):
    return pl.ds(pl.multiple_of(index * size, size), size)


def gather_kernel(planes, groups, q_ref, k_ref, v_ref, g_ref, qo_ref, go_ref, kv_ref,
                  local, a2a_send, a2a_recv, z_send, z_recv, sib_send, sib_recv):
    at = Where(planes, groups)
    rows = q_ref.shape[0]
    wide = q_ref.shape[1] // (NS * groups)
    half_rows = kv_ref.shape[2] // 2
    mine = aligned(at.p, rows)
    cols_own = aligned(at.g, HD)

    own_q = pltpu.make_async_copy(q_ref.at[:, aligned(at.g * NS + at.s, wide)], qo_ref.at[mine], local.at[0])
    own_g = pltpu.make_async_copy(g_ref.at[:, aligned(at.g * NS + at.s, wide)], go_ref.at[mine], local.at[1])
    own_k = pltpu.make_async_copy(k_ref.at[:, cols_own], kv_ref.at[0, at.z, mine], local.at[2])
    own_v = pltpu.make_async_copy(v_ref.at[:, cols_own], kv_ref.at[1, at.z, mine], local.at[2])
    own_q.start()
    own_g.start()

    @pl.when(at.core == 0)
    def _():
        own_k.start()

    @pl.when(at.core == 1)
    def _():
        own_v.start()

    at.greet()

    def send_kv(i, carry):
        _, os, og, device = at.peer(i)
        cols = aligned(og, HD)

        @pl.when(os % 2 == 0)
        def _():
            remote(k_ref.at[:, cols], kv_ref.at[0, at.z, mine], a2a_send.at[0], a2a_recv.at[0], device).start()

        @pl.when(os % 2 == 1)
        def _():
            remote(v_ref.at[:, cols], kv_ref.at[1, at.z, mine], a2a_send.at[0], a2a_recv.at[0], device).start()

        return carry

    lax.fori_loop(1, at.size, send_kv, 0)

    def send_q(i, carry):
        _, os, og, device = at.peer(i)
        cols = aligned(og * NS + os, wide)
        remote(q_ref.at[:, cols], qo_ref.at[mine], a2a_send.at[1], a2a_recv.at[1], device).start()
        remote(g_ref.at[:, cols], go_ref.at[mine], a2a_send.at[2], a2a_recv.at[2], device).start()
        return carry

    lax.fori_loop(1, at.size, send_q, 0)

    others = pl.ds(0, rows * (at.size - 1))
    own_k.wait()
    got = kv_ref.at[at.core, at.z, others]
    remote(got, got, a2a_send.at[0], a2a_recv.at[0], at.up).wait_recv()

    def piece(chunk, half):
        return kv_ref.at[at.core, chunk, pl.ds(half * half_rows, half_rows)]

    own = kv_ref.at[at.core, at.z]
    hops = planes // 2

    def moves(j, half, way):
        return j < hops - 1 or half == way

    def chunk_at(j, way):
        return (at.z + planes - j) % planes if way == 0 else (at.z + j) % planes

    def send(j, half, way):
        ref = piece(chunk_at(j, way), half)
        slot = (way, 2 * j + half)
        return remote(ref, ref, z_send.at[slot], z_recv.at[slot], at.up if way == 0 else at.down)

    def arrival(j, half, way):
        ref = piece(chunk_at(j + 1, way), half)
        slot = (way, 2 * j + half)
        return remote(ref, ref, z_send.at[slot], z_recv.at[slot], at.up if way == 0 else at.down)

    for j in range(hops):
        for half in (0, 1):
            for way in (0, 1):
                if j > 0:
                    arrival(j - 1, half, way).wait_recv()
                if moves(j, half, way):
                    send(j, half, way).start()
                if j > 0:
                    ref = piece(chunk_at(j, way), half)
                    remote(ref, ref, sib_send, sib_recv, at.sib).start()
        if j == 0:
            remote(own, own, sib_send, sib_recv, at.sib).start()
    for way in (0, 1):
        arrival(hops - 1, way, way).wait_recv()
        ref = piece(chunk_at(hops, way), way)
        remote(ref, ref, sib_send, sib_recv, at.sib).start()

    own_q.wait()
    own_g.wait()
    for n, (src, dst) in enumerate(((q_ref, qo_ref), (g_ref, go_ref))):
        sent = src.at[:, pl.ds(0, wide * (at.size - 1))]
        came = dst.at[others]
        remote(came, came, a2a_send.at[n + 1], a2a_recv.at[n + 1], at.up).wait_recv()
        remote(sent, sent, a2a_send.at[n + 1], a2a_recv.at[n + 1], at.up).wait_send()
    remote(got, got, a2a_send.at[0], a2a_recv.at[0], at.up).wait_send()
    for j in range(hops):
        for half in (0, 1):
            for way in (0, 1):
                if moves(j, half, way):
                    send(j, half, way).wait_send()
    sent = kv_ref.at[at.core]
    came = kv_ref.at[1 - at.core]
    remote(sent, sent, sib_send, sib_recv, at.sib).wait_send()
    remote(came, came, sib_send, sib_recv, at.sib).wait_recv()


def gather(planes, groups, queries, keys, values, out_grad):
    rows = queries.shape[0]
    plane_rows = rows * NS * groups
    wide = queries.shape[1] // (NS * groups)
    hops = planes // 2
    any_space = pl.BlockSpec(memory_space=pl.ANY)
    return pl.pallas_call(
        functools.partial(gather_kernel, planes, groups),
        out_shape=(
            jax.ShapeDtypeStruct((plane_rows, wide), BF16),
            jax.ShapeDtypeStruct((plane_rows, wide), BF16),
            jax.ShapeDtypeStruct((2, planes, plane_rows, HD), BF16),
        ),
        in_specs=[any_space] * 4,
        out_specs=(any_space,) * 3,
        scratch_shapes=[
            pltpu.SemaphoreType.DMA((3,)),
            pltpu.SemaphoreType.DMA((3,)),
            pltpu.SemaphoreType.DMA((3,)),
            pltpu.SemaphoreType.DMA((2, 2 * hops)),
            pltpu.SemaphoreType.DMA((2, 2 * hops)),
            pltpu.SemaphoreType.DMA,
            pltpu.SemaphoreType.DMA,
        ],
        compiler_params=pltpu.CompilerParams(
            collective_id=0, has_side_effects=True, vmem_limit_bytes=VMEM_LIMIT
        ),
        name="gather",
    )(queries, keys, values, out_grad)


def attend_kernel(order_ref, doc_ref, plane_ref, doc2_ref, q_ref, g_ref, kv_ref, att_ref, dq_ref, dkv_ref,
                  q_s, g_s, att_s, dq_s, kv_s, kvt_s, dkv_s, out_s, s_s, p_s, acc_s, top_s, total_s,
                  begin_s, start_s, sem):
    tokens = kv_ref.shape[1]
    blocks = tokens // BLK
    own_blocks = q_ref.shape[0] // BLK
    heads = q_ref.shape[1] // HD
    rows = heads * BLK
    turned = min(tokens, 2048)

    def fetch(i, carry):
        dst = pl.ds(pl.multiple_of(FRONT + order_ref[i] * BLK, BLK), BLK)
        pltpu.make_async_copy(kv_ref.at[:, aligned(i, BLK)], kv_s.at[:, dst], sem.at[0]).start()
        return carry

    lax.fori_loop(0, blocks, fetch, 0)
    load_q = pltpu.make_async_copy(q_ref, q_s, sem.at[2])
    load_g = pltpu.make_async_copy(g_ref, g_s, sem.at[3])
    load_q.start()
    load_g.start()
    head = pl.ds(0, FRONT)
    kv_s[:, head, :] = jnp.zeros((2, FRONT, HD), BF16)
    kvt_s[:, :, head] = jnp.zeros((2, HD, FRONT), BF16)
    dkv_s[:, head, :] = jnp.zeros((2, FRONT, HD), F32)

    def clear(i, carry):
        at = pl.ds(pl.multiple_of(FRONT + i * 512, BLK), 512)
        dkv_s[:, at, :] = jnp.zeros((2, 512, HD), F32)
        return carry

    lax.fori_loop(0, tokens // 512, clear, 0)

    def eye(n):
        return (lax.broadcasted_iota(jnp.int32, (n, n), 0) == lax.broadcasted_iota(jnp.int32, (n, n), 1)).astype(
            F32).astype(BF16)

    eye_d = eye(HD)
    eye_r = eye(rows)
    packed = [order_ref[plane_ref[0] * own_blocks + n] for n in range(own_blocks)]
    firsts = [b * BLK for b in packed]
    wanted = [doc_ref[first] for first in firsts]

    def halve(_, spans):
        lows, highs = [], []
        for (lo, hi), doc0 in zip(spans, wanted):
            mid = (lo + hi) // 2
            below = doc_ref[mid] < doc0
            lows.append(jnp.where(below, mid + 1, lo))
            highs.append(jnp.where(below, hi, mid))
        return tuple(zip(lows, highs))

    spans = lax.fori_loop(0, tokens.bit_length(), halve, tuple((jnp.int32(0), first) for first in firsts))
    starts = [lo for lo, _ in spans]
    for n in range(own_blocks):
        start_s[n] = starts[n]
    lane = lax.broadcasted_iota(jnp.int32, (own_blocks, BLK), 1)
    docs = jnp.concatenate([doc2_ref[pl.ds(b, 1), :] for b in packed], axis=0)
    opens = (lane > 0) & (docs != pltpu.roll(docs, 1, 1))
    first_of = jnp.concatenate([jnp.full((1, BLK), first, jnp.int32) for first in firsts], axis=0)
    start_of = jnp.concatenate([jnp.full((1, BLK), start, jnp.int32) for start in starts], axis=0)
    begin = jnp.where(opens, first_of + lane, start_of)
    step = 1
    while step < BLK:
        begin = jnp.maximum(begin, jnp.where(lane >= step, pltpu.roll(begin, step, 1), 0))
        step *= 2
    begin_s[...] = begin
    pltpu.make_async_copy(kv_ref, kv_s.at[:, pl.ds(FRONT, tokens)], sem.at[0]).wait()

    def turn(i, carry):
        at = pl.ds(pl.multiple_of(FRONT + i * turned, BLK), turned)
        kvt_s[0, :, at] = dot(eye_d, kv_s[0, at, :], NT).astype(BF16)
        kvt_s[1, :, at] = dot(eye_d, kv_s[1, at, :], NT).astype(BF16)
        return carry

    lax.fori_loop(0, tokens // turned, turn, 0)

    def query_block(n, carry):
        packed = order_ref[plane_ref[0] * own_blocks + n]
        first = packed * BLK
        doc_start = start_s[n]
        pairs = (first // BLK - doc_start // BLK + PAIR // BLK) // (PAIR // BLK)
        base = FRONT + first + BLK - pairs * PAIR
        lead = (pairs - 1) % (KTILE // PAIR) + 1
        tiles = (pairs - 1) // (KTILE // PAIR)

        def each_tile(work):
            for size in range(1, KTILE // PAIR + 1):
                @pl.when(lead == size)
                def _():
                    work(0, size * PAIR, True)

            def step(t, carry):
                work(pl.multiple_of(lead * PAIR + t * KTILE, PAIR), KTILE, False)
                return carry

            lax.fori_loop(0, tiles, step, 0)

        begin = begin_s[pl.ds(n, 1), :]
        lane = lax.broadcasted_iota(jnp.int32, (1, BLK), 1)
        bias = jnp.where(begin > doc_start, NEG, 0.0)
        bias = jnp.concatenate([bias] * heads, axis=1)
        low = jnp.concatenate([begin] * heads, axis=1) + (FRONT - base)
        high = jnp.concatenate([first + lane] * heads, axis=1) + (FRONT - base)

        here = aligned(n, BLK)
        qs = jnp.concatenate([q_s[here, h * HD:(h + 1) * HD] for h in range(heads)], axis=0)
        gs = jnp.concatenate([g_s[here, h * HD:(h + 1) * HD] for h in range(heads)], axis=0)

        def score_tile(rel, width, leads):
            score = dot(kv_s[0, pl.ds(pl.multiple_of(base + rel, BLK), width), :], qs, NT)
            cuts = [(0, PAIR, True)] if leads else []
            if leads and width > PAIR:
                cuts += [(PAIR, width - BLK, False), (width - BLK, width, True)]
            elif not leads:
                cuts = [(0, width - BLK, False), (width - BLK, width, True)]
            top = None
            for start, end, edge in cuts:
                count = end - start
                part = score[start:end] * (SCALE * LOG2E)
                if edge:
                    key_at = lax.broadcasted_iota(jnp.int32, (count, rows), 0)
                    seen = (key_at >= low - (rel + start)) & (key_at <= high - (rel + start))
                    part = jnp.where(seen, part, NEG)
                else:
                    part = part + bias
                s_s[pl.ds(pl.multiple_of(rel + start, BLK), count), :] = part
                most = jnp.max(part.reshape(count // LANES, LANES, rows), axis=0)
                top = most if top is None else jnp.maximum(top, most)
            top_s[...] = top if leads else jnp.maximum(top_s[...], top)

        each_tile(score_tile)
        top = jnp.max(top_s[...], axis=0, keepdims=True)

        def prob_tile(rel, width, leads):
            at = pl.ds(pl.multiple_of(base + rel, BLK), width)
            there = pl.ds(pl.multiple_of(rel, PAIR), width)
            prob = jnp.exp2(s_s[there, :] - top)
            rounded = prob.astype(BF16)
            p_s[there, :] = rounded
            part = dot(kvt_s[1, :, at], rounded, NN)
            total = jnp.sum(prob.reshape(width // LANES, LANES, rows), axis=0)
            if leads:
                acc_s[...] = part
                total_s[...] = total
            else:
                acc_s[...] += part
                total_s[...] += total

        each_tile(prob_tile)
        inverse = 1.0 / jnp.sum(total_s[...], axis=0, keepdims=True)
        att_t = (acc_s[...] * inverse).astype(BF16)
        g_t = dot(eye_d, gs, NT)
        q_t = dot(eye_d, qs, NT)
        delta = jnp.sum(g_t * att_t.astype(F32), axis=0, keepdims=True)
        g_n = (g_t * inverse).astype(BF16)
        q_n = (q_t * (inverse * SCALE)).astype(BF16)
        att = dot(eye_r, att_t, NT).astype(BF16)
        for h in range(heads):
            att_s[here, h * HD:(h + 1) * HD] = att[h * BLK:(h + 1) * BLK]

        def grad_tile(rel, width, leads):
            at = pl.ds(pl.multiple_of(base + rel, BLK), width)
            prob = p_s[pl.ds(pl.multiple_of(rel, PAIR), width), :]
            dprob = dot(kv_s[1, at, :], gs, NT)
            dscore = (prob.astype(F32) * (dprob - delta)).astype(BF16)
            dkv_s[1, at, :] += dot(prob, g_n, NT)
            dkv_s[0, at, :] += dot(dscore, q_n, NT)
            part = dot(kvt_s[0, :, at], dscore, NN)
            if leads:
                acc_s[...] = part
            else:
                acc_s[...] += part

        each_tile(grad_tile)
        dq_t = (acc_s[...] * (inverse * SCALE)).astype(BF16)
        dq = dot(eye_r, dq_t, NT).astype(BF16)
        for h in range(heads):
            dq_s[here, h * HD:(h + 1) * HD] = dq[h * BLK:(h + 1) * BLK]
        pltpu.make_async_copy(att_s.at[here], att_ref.at[here], sem.at[2]).start()
        pltpu.make_async_copy(dq_s.at[here], dq_ref.at[here], sem.at[3]).start()
        return carry

    load_q.wait()
    load_g.wait()
    lax.fori_loop(0, own_blocks, query_block, 0)

    def hand_out(i, carry):
        for j in range(OUT):
            src = pl.ds(pl.multiple_of(FRONT + order_ref[i * OUT + j] * BLK, BLK), BLK)
            dst = aligned(i * OUT + j, BLK)
            out_s[:, dst, :] = dkv_s[:, src, :].astype(BF16)
        dst = aligned(i, OUT * BLK)
        pltpu.make_async_copy(out_s.at[:, dst], dkv_ref.at[:, dst], sem.at[1]).start()
        return carry

    lax.fori_loop(0, blocks // OUT, hand_out, 0)
    pltpu.make_async_copy(att_s, att_ref, sem.at[2]).wait()
    pltpu.make_async_copy(dq_s, dq_ref, sem.at[3]).wait()
    pltpu.make_async_copy(out_s, dkv_ref, sem.at[1]).wait()


def attend(plane, q_loc, g_loc, kv, doc_ids, block_order):
    tokens = kv.shape[1]
    rows = q_loc.shape[1] // HD * BLK
    padded = FRONT + tokens
    longest = (min(tokens, 4096) + BLK + PAIR - 1) // PAIR * PAIR
    vmem = pl.BlockSpec(memory_space=pltpu.VMEM)
    smem = pl.BlockSpec(memory_space=pltpu.SMEM)
    any_space = pl.BlockSpec(memory_space=pl.ANY)
    return pl.pallas_call(
        attend_kernel,
        out_shape=(
            jax.ShapeDtypeStruct(q_loc.shape, BF16),
            jax.ShapeDtypeStruct(q_loc.shape, BF16),
            jax.ShapeDtypeStruct(kv.shape, BF16),
        ),
        in_specs=[smem, smem, smem, vmem, any_space, any_space, any_space],
        out_specs=(any_space,) * 3,
        scratch_shapes=[
            pltpu.VMEM(q_loc.shape, BF16),
            pltpu.VMEM(q_loc.shape, BF16),
            pltpu.VMEM(q_loc.shape, BF16),
            pltpu.VMEM(q_loc.shape, BF16),
            pltpu.VMEM((2, padded, HD), BF16),
            pltpu.VMEM((2, HD, padded), BF16),
            pltpu.VMEM((2, padded, HD), F32),
            pltpu.VMEM((2, tokens, HD), BF16),
            pltpu.VMEM((longest, rows), F32),
            pltpu.VMEM((longest, rows), BF16),
            pltpu.VMEM((HD, rows), F32),
            pltpu.VMEM((LANES, rows), F32),
            pltpu.VMEM((LANES, rows), F32),
            pltpu.VMEM((q_loc.shape[0] // BLK, BLK), jnp.int32),
            pltpu.SMEM((q_loc.shape[0] // BLK,), jnp.int32),
            pltpu.SemaphoreType.DMA((4,)),
        ],
        compiler_params=pltpu.CompilerParams(vmem_limit_bytes=VMEM_LIMIT),
        name="attend",
    )(block_order, doc_ids, plane, doc_ids.reshape(tokens // BLK, BLK), q_loc, g_loc, kv)


def scatter_kernel(planes, groups, att_ref, dq_ref, dkv_ref, ao_ref, dqo_ref, land_s,
                   mine_s, sib_s, stage_s, came_s, fin_s,
                   local, mine_sem, sib_send, sib_recv, a2a_send, a2a_recv, z_send, z_recv):
    at = Where(planes, groups)
    rows = ao_ref.shape[0]
    wide = att_ref.shape[1]
    half_rows = dkv_ref.shape[2] // 2
    hops = planes // 2
    mine = aligned(at.p, rows)
    cols = aligned(at.g * NS + at.s, wide)

    own_a = pltpu.make_async_copy(att_ref.at[mine], ao_ref.at[:, cols], local.at[0])
    own_q = pltpu.make_async_copy(dq_ref.at[mine], dqo_ref.at[:, cols], local.at[1])
    own_a.start()
    own_q.start()

    turns = [hops]
    for j in range(hops - 1, 0, -1):
        turns += [j, -j]
    turns += [0]
    own_part, sib_part = [], []
    for n, distance in enumerate(turns):
        chunk = (at.z + planes + distance) % planes
        own_part.append(pltpu.make_async_copy(dkv_ref.at[at.core, chunk], mine_s.at[chunk], mine_sem.at[n]))
        sib_part.append(remote(dkv_ref.at[1 - at.core, chunk], sib_s.at[chunk],
                               sib_send.at[n], sib_recv.at[n], at.sib))
    for copy in own_part:
        copy.start()
    at.greet()
    for copy in sib_part:
        copy.start()

    def send_out(i, carry):
        o, _, _, device = at.peer(i)
        theirs = aligned(o, rows)
        remote(att_ref.at[theirs], ao_ref.at[:, cols], a2a_send.at[0], a2a_recv.at[0], device).start()
        remote(dq_ref.at[theirs], dqo_ref.at[:, cols], a2a_send.at[1], a2a_recv.at[1], device).start()
        return carry

    lax.fori_loop(1, at.size, send_out, 0)

    def ready(distance):
        n = turns.index(distance)
        own_part[n].wait()
        sib_part[n].wait_recv()

    def own_sum(distance, half):
        chunk = (at.z + planes + distance) % planes
        part = pl.ds(half * half_rows, half_rows)
        return mine_s[chunk, part, :].astype(F32) + sib_s[chunk, part, :].astype(F32)

    def moves(j, half, way):
        return j > 0 or half == way

    def send(j, half, way):
        slot = (way, 2 * j + half)
        return remote(stage_s.at[slot], came_s.at[slot], z_send.at[slot], z_recv.at[slot],
                      at.up if way == 0 else at.down)

    for j in range(hops):
        distance = hops - j
        if j == 0:
            ready(hops)
        else:
            ready(distance)
            ready(-distance)
        for turn in (0, 1):
            for way in (0, 1):
                half = 1 - way if turn == 0 else way
                if not moves(j, half, way):
                    continue
                value = own_sum(distance if way == 0 else -distance, half)
                if j > 0 and moves(j - 1, half, way):
                    send(j - 1, half, way).wait_recv()
                    value = value + came_s[way, 2 * (j - 1) + half].astype(F32)
                stage_s[way, 2 * j + half] = value.astype(BF16)
                send(j, half, way).start()

    ready(0)
    for half in (0, 1):
        value = own_sum(0, half)
        for way in (0, 1):
            if moves(hops - 1, half, way):
                send(hops - 1, half, way).wait_recv()
                value = value + came_s[way, 2 * (hops - 1) + half].astype(F32)
        fin_s[pl.ds(half * half_rows, half_rows), :] = value.astype(BF16)

    group_cols = aligned(at.g, HD)
    target = land_s.at[at.core, at.ylo, :, group_cols]
    own_fin = pltpu.make_async_copy(fin_s.at[mine], target, local.at[2])
    own_fin.start()

    def send_fin(i, carry):
        o, _, _, device = at.peer(i)
        remote(fin_s.at[aligned(o, rows)], target, a2a_send.at[2], a2a_recv.at[2], device).start()
        return carry

    lax.fori_loop(1, at.size, send_fin, 0)

    others = pl.ds(0, rows * (at.size - 1))
    some = pl.ds(0, wide * (at.size - 1))
    own_a.wait()
    own_q.wait()
    for n, (src, dst) in enumerate(((att_ref, ao_ref), (dq_ref, dqo_ref))):
        sent, came = src.at[others], dst.at[:, some]
        remote(came, came, a2a_send.at[n], a2a_recv.at[n], at.up).wait_recv()
        remote(sent, sent, a2a_send.at[n], a2a_recv.at[n], at.up).wait_send()
    for j in range(hops):
        for half in (0, 1):
            for way in (0, 1):
                if moves(j, half, way):
                    send(j, half, way).wait_send()
    for copy in sib_part:
        copy.wait_send()
    own_fin.wait()
    moved = fin_s.at[others]
    remote(moved, moved, a2a_send.at[2], a2a_recv.at[2], at.up).wait()


def scatter(planes, groups, att, dq, dkv):
    plane_rows = att.shape[0]
    rows = plane_rows // (NS * groups)
    columns = att.shape[1] * NS * groups
    hops = planes // 2
    any_space = pl.BlockSpec(memory_space=pl.ANY)
    dma = pltpu.SemaphoreType.DMA
    return pl.pallas_call(
        functools.partial(scatter_kernel, planes, groups),
        out_shape=(
            jax.ShapeDtypeStruct((rows, columns), BF16),
            jax.ShapeDtypeStruct((rows, columns), BF16),
            jax.ShapeDtypeStruct((2, NS // 2, rows, groups * HD), BF16),
        ),
        in_specs=[any_space] * 3,
        out_specs=(any_space,) * 3,
        scratch_shapes=[
            pltpu.VMEM((planes, plane_rows, HD), BF16),
            pltpu.VMEM((planes, plane_rows, HD), BF16),
            pltpu.VMEM((2, 2 * hops, plane_rows // 2, HD), BF16),
            pltpu.VMEM((2, 2 * hops, plane_rows // 2, HD), BF16),
            pltpu.VMEM((plane_rows, HD), BF16),
            dma((3,)),
            dma((planes,)),
            dma((planes,)),
            dma((planes,)),
            dma((3,)),
            dma((3,)),
            dma((2, 2 * hops)),
            dma((2, 2 * hops)),
        ],
        compiler_params=pltpu.CompilerParams(
            collective_id=1, has_side_effects=True, vmem_limit_bytes=VMEM_LIMIT
        ),
        name="scatter",
    )(att, dq, dkv)


def finish_kernel(a_ref, q_ref, land_ref, ao_ref, qo_ref, kg_ref, vg_ref, sem):
    moves = [pltpu.make_async_copy(a_ref, ao_ref, sem.at[0]), pltpu.make_async_copy(q_ref, qo_ref, sem.at[1])]
    for move in moves:
        move.start()
    for part, out in ((0, kg_ref), (1, vg_ref)):
        total = land_ref[part, 0].astype(F32)
        for ylo in range(1, NS // 2):
            total = total + land_ref[part, ylo].astype(F32)
        out[...] = total.astype(BF16)
    for move in moves:
        move.wait()


def finish(att, dq, land):
    any_space = pl.BlockSpec(memory_space=pl.ANY)
    vmem = pl.BlockSpec(memory_space=pltpu.VMEM)
    grad = jax.ShapeDtypeStruct(land.shape[2:], BF16)
    return pl.pallas_call(
        finish_kernel,
        out_shape=(jax.ShapeDtypeStruct(att.shape, BF16), jax.ShapeDtypeStruct(dq.shape, BF16), grad, grad),
        in_specs=[vmem, vmem, vmem],
        out_specs=(any_space, any_space, vmem, vmem),
        scratch_shapes=[pltpu.SemaphoreType.DMA((2,))],
        name="finish",
    )(att, dq, land)


def per_device(planes, groups, queries, keys, values, out_grad, doc_ids, block_order):
    plane = (lax.axis_index("ctx") // NS).astype(jnp.int32).reshape(1)
    q_loc, g_loc, kv = gather(planes, groups, queries, keys, values, out_grad)
    tokens = doc_ids.shape[0]
    att, dq, dkv = attend(plane, q_loc, g_loc, kv.reshape(2, tokens, HD), doc_ids, block_order)
    return finish(*scatter(planes, groups, att, dq, dkv.reshape(kv.shape)))


def solution(mesh):
    split = P(("ctx", "head"), None)
    planes, groups = mesh.shape["ctx"] // NS, mesh.shape["head"]
    return jax.shard_map(
        functools.partial(per_device, planes, groups),
        mesh=mesh,
        in_specs=(split, split, split, split, P(), P()),
        out_specs=(split, split, split, split),
        check_vma=False,
    )
```

```python
import functools
import math

import jax
import jax.numpy as jnp
from jax import lax
from jax.experimental import pallas as pl
from jax.experimental.pallas import tpu as pltpu
from jax.sharding import PartitionSpec as P

QH = 64
KVH = 8
HD = 128
BLK = 128
NS = 4
KTILE = 2048
PAIR = 2 * BLK
LANES = 32
OUT = 8
UNITS = 4
ALONE = 1
CARRIED = UNITS - ALONE
OUT_AT = 0
PIECES = 4
FIRST_WAY = (0,)
FRONT = BLK
LOG2E = math.log2(math.e)
SCALE = 1.0 / math.sqrt(HD)
NEG = -1e30
MESH = pl.DeviceIdType.MESH
F32 = jnp.float32
BF16 = jnp.bfloat16
NT = (((1,), (1,)), ((), ()))
NN = (((1,), (0,)), ((), ()))
VMEM_LIMIT = 56 * 1024 * 1024


def dot(a, b, dims):
    return lax.dot_general(a, b, dims, preferred_element_type=F32)


class Where:
    def __init__(self, planes, groups):
        ctx = lax.axis_index("ctx")
        self.planes, self.groups = planes, groups
        self.size = NS * groups
        self.g = lax.axis_index("head")
        self.z, self.s = ctx // NS, ctx % NS
        self.core, self.ylo = self.s % 2, self.s // 2
        self.p = self.s * groups + self.g
        self.up = (((self.z + 1) % planes) * NS + self.s, self.g)
        self.down = (((self.z + planes - 1) % planes) * NS + self.s, self.g)
        self.sib = (ctx + 1 - 2 * self.core, self.g)
        self.other = (self.z * NS + lax.rem(self.s + 2, NS), self.g)

        self.slots = [lax.rem(self.s + a, NS) for a in range(NS)]
        self.ranks = [lax.rem(self.g + b, groups) for b in range(groups)]
        self.lines = [self.z * NS + slot for slot in self.slots]

    def unit(self, r):
        return self.ylo * CARRIED + r if r < ALONE else r

    def others_unit(self, r):
        return (1 - self.ylo) * CARRIED + r

    def peers(self, a):
        return [(self.slots[a], rank, (self.lines[a], rank)) for b, rank in enumerate(self.ranks) if (a, b) != (0, 0)]

    def each_peer(self, work):
        for a in range(NS):

            def step(b, carry):
                rank = lax.rem(self.g + b, self.groups)
                work(self.slots[a], rank, (self.lines[a], rank))
                return carry

            lax.fori_loop(0 if a else 1, self.groups, step, 0)

    def greet(self):
        bar = pltpu.get_barrier_semaphore()
        for a in range(NS):
            for _, _, device in self.peers(a):
                pl.semaphore_signal(bar, inc=1, device_id=device, device_id_type=MESH)
        for other in (self.up, self.down):
            pl.semaphore_signal(bar, inc=1, device_id=other, device_id_type=MESH)
        pl.semaphore_wait(bar, self.size + 1)


def remote(src, dst, send, recv, device):
    return pltpu.make_async_remote_copy(
        src_ref=src, dst_ref=dst, send_sem=send, recv_sem=recv, device_id=device, device_id_type=MESH
    )


def aligned(index, size):
    return pl.ds(pl.multiple_of(index * size, size), size)


def gather_kernel(planes, groups, q_ref, k_ref, v_ref, g_ref, qo_ref, go_ref, kv_ref,
                  local, a2a_send, a2a_recv, z_send, z_recv, y_send, y_recv, sib_send, sib_recv):
    at = Where(planes, groups)
    rows = q_ref.shape[0]
    wide = q_ref.shape[1] // (NS * groups)
    unit_rows = kv_ref.shape[2] // UNITS
    mine = aligned(at.p, rows)
    cols_own = aligned(at.g, HD)

    own_q = pltpu.make_async_copy(q_ref.at[:, aligned(at.g * NS + at.s, wide)], qo_ref.at[mine], local.at[0])
    own_g = pltpu.make_async_copy(g_ref.at[:, aligned(at.g * NS + at.s, wide)], go_ref.at[mine], local.at[1])
    own_k = pltpu.make_async_copy(k_ref.at[:, cols_own], kv_ref.at[0, at.z, mine], local.at[2])
    own_v = pltpu.make_async_copy(v_ref.at[:, cols_own], kv_ref.at[1, at.z, mine], local.at[2])
    own_q.start()
    own_g.start()

    @pl.when(at.core == 0)
    def _():
        own_k.start()

    @pl.when(at.core == 1)
    def _():
        own_v.start()

    at.greet()

    for a in range(NS):
        for kind, source in ((0, k_ref), (1, v_ref)):
            @pl.when(lax.rem(at.core + a, 2) == kind)
            def _():
                for _, og, device in at.peers(a):
                    remote(source.at[:, aligned(og, HD)], kv_ref.at[kind, at.z, mine],
                           a2a_send.at[0], a2a_recv.at[0], device).start()

    def send_q(os, og, device):
        cols = aligned(og * NS + os, wide)
        remote(q_ref.at[:, cols], qo_ref.at[mine], a2a_send.at[1], a2a_recv.at[1], device).start()
        remote(g_ref.at[:, cols], go_ref.at[mine], a2a_send.at[2], a2a_recv.at[2], device).start()

    others = pl.ds(0, rows * (at.size - 1))
    own_k.wait()
    got = kv_ref.at[at.core, at.z, others]
    remote(got, got, a2a_send.at[0], a2a_recv.at[0], at.up).wait_recv()

    def piece(chunk, unit):
        return kv_ref.at[at.core, chunk, pl.ds(pl.multiple_of(unit * unit_rows, unit_rows), unit_rows)]

    own = kv_ref.at[at.core, at.z]
    hops = planes // 2

    def moves(j, r, way):
        return j < hops - 1 or (r in FIRST_WAY) == (way == 0)

    def chunk_at(j, way):
        return (at.z + planes - j) % planes if way == 0 else (at.z + j) % planes

    def send(j, r, way):
        ref = piece(chunk_at(j, way), at.unit(r))
        slot = (way, CARRIED * j + r)
        return remote(ref, ref, z_send.at[slot], z_recv.at[slot], at.up if way == 0 else at.down)

    def arrival(j, r, way):
        ref = piece(chunk_at(j + 1, way), at.unit(r))
        slot = (way, CARRIED * j + r)
        return remote(ref, ref, z_send.at[slot], z_recv.at[slot], at.up if way == 0 else at.down)

    def across(j, r, way, unit):
        ref = piece(chunk_at(j + 1, way), unit)
        slot = (way, ALONE * j + r)
        return remote(ref, ref, y_send.at[slot], y_recv.at[slot], at.other)

    def to_sib(ref):
        remote(ref, ref, sib_send, sib_recv, at.sib).start()

    def take_across(j):
        for r in range(ALONE):
            for way in (0, 1):
                if moves(j, r, way):
                    across(j, r, way, at.others_unit(r)).wait_recv()
                    to_sib(piece(chunk_at(j + 1, way), at.others_unit(r)))

    for j in range(hops + 1):
        for r in range(CARRIED):
            for way in (0, 1):
                if j > 0:
                    if not moves(j - 1, r, way):
                        continue
                    arrival(j - 1, r, way).wait_recv()
                if j < hops and moves(j, r, way):
                    send(j, r, way).start()
                if j > 0:
                    if r < ALONE:
                        across(j - 1, r, way, at.unit(r)).start()
                    to_sib(piece(chunk_at(j, way), at.unit(r)))
        if j == 0:
            to_sib(own)
            at.each_peer(send_q)
        if j > 1:
            take_across(j - 2)
    take_across(hops - 1)

    own_q.wait()
    own_g.wait()
    for n, (src, dst) in enumerate(((q_ref, qo_ref), (g_ref, go_ref))):
        sent = src.at[:, pl.ds(0, wide * (at.size - 1))]
        came = dst.at[others]
        remote(came, came, a2a_send.at[n + 1], a2a_recv.at[n + 1], at.up).wait_recv()
        remote(sent, sent, a2a_send.at[n + 1], a2a_recv.at[n + 1], at.up).wait_send()
    remote(got, got, a2a_send.at[0], a2a_recv.at[0], at.up).wait_send()
    for j in range(hops):
        for r in range(CARRIED):
            for way in (0, 1):
                if moves(j, r, way):
                    send(j, r, way).wait_send()
                    if r < ALONE:
                        across(j, r, way, at.unit(r)).wait_send()
    sent = kv_ref.at[at.core]
    came = kv_ref.at[1 - at.core]
    remote(sent, sent, sib_send, sib_recv, at.sib).wait_send()
    remote(came, came, sib_send, sib_recv, at.sib).wait_recv()


def gather(planes, groups, queries, keys, values, out_grad):
    rows = queries.shape[0]
    plane_rows = rows * NS * groups
    wide = queries.shape[1] // (NS * groups)
    hops = planes // 2
    any_space = pl.BlockSpec(memory_space=pl.ANY)
    return pl.pallas_call(
        functools.partial(gather_kernel, planes, groups),
        out_shape=(
            jax.ShapeDtypeStruct((plane_rows, wide), BF16),
            jax.ShapeDtypeStruct((plane_rows, wide), BF16),
            jax.ShapeDtypeStruct((2, planes, plane_rows, HD), BF16),
        ),
        in_specs=[any_space] * 4,
        out_specs=(any_space,) * 3,
        scratch_shapes=[
            pltpu.SemaphoreType.DMA((3,)),
            pltpu.SemaphoreType.DMA((3,)),
            pltpu.SemaphoreType.DMA((3,)),
            pltpu.SemaphoreType.DMA((2, CARRIED * hops)),
            pltpu.SemaphoreType.DMA((2, CARRIED * hops)),
            pltpu.SemaphoreType.DMA((2, ALONE * hops)),
            pltpu.SemaphoreType.DMA((2, ALONE * hops)),
            pltpu.SemaphoreType.DMA,
            pltpu.SemaphoreType.DMA,
        ],
        compiler_params=pltpu.CompilerParams(
            collective_id=0, has_side_effects=True, vmem_limit_bytes=VMEM_LIMIT
        ),
        name="gather",
    )(queries, keys, values, out_grad)


def attend_kernel(order_ref, doc_ref, plane_ref, doc2_ref, q_ref, g_ref, kv_ref, att_ref, dq_ref, dkv_ref,
                  q_s, g_s, att_s, dq_s, kv_s, kvt_s, dkv_s, out_s, s_s, p_s, acc_s, top_s, total_s,
                  begin_s, start_s, sem):
    tokens = kv_ref.shape[1]
    blocks = tokens // BLK
    own_blocks = q_ref.shape[0] // BLK
    heads = q_ref.shape[1] // HD
    rows = heads * BLK
    turned = min(tokens, 4096)

    def fetch(i, carry):
        dst = pl.ds(pl.multiple_of(FRONT + order_ref[i] * BLK, BLK), BLK)
        pltpu.make_async_copy(kv_ref.at[:, aligned(i, BLK)], kv_s.at[:, dst], sem.at[0]).start()
        return carry

    lax.fori_loop(0, blocks, fetch, 0)
    load_q = pltpu.make_async_copy(q_ref, q_s, sem.at[2])
    load_g = pltpu.make_async_copy(g_ref, g_s, sem.at[3])
    load_q.start()
    load_g.start()
    head = pl.ds(0, FRONT)
    kv_s[:, head, :] = jnp.zeros((2, FRONT, HD), BF16)
    kvt_s[:, :, head] = jnp.zeros((2, HD, FRONT), BF16)
    dkv_s[:, head, :] = jnp.zeros((2, FRONT, HD), F32)

    def clear(i, carry):
        at = pl.ds(pl.multiple_of(FRONT + i * 512, BLK), 512)
        dkv_s[:, at, :] = jnp.zeros((2, 512, HD), F32)
        return carry

    lax.fori_loop(0, tokens // 512, clear, 0)

    def eye(n):
        return (lax.broadcasted_iota(jnp.int32, (n, n), 0) == lax.broadcasted_iota(jnp.int32, (n, n), 1)).astype(
            F32).astype(BF16)

    eye_d = eye(HD)
    eye_r = eye(rows)
    packed = [order_ref[plane_ref[0] * own_blocks + n] for n in range(own_blocks)]
    firsts = [b * BLK for b in packed]
    wanted = [doc_ref[first] for first in firsts]

    def halve(_, spans):
        lows, highs = [], []
        for (lo, hi), doc0 in zip(spans, wanted):
            mid = (lo + hi) // 2
            below = doc_ref[mid] < doc0
            lows.append(jnp.where(below, mid + 1, lo))
            highs.append(jnp.where(below, hi, mid))
        return tuple(zip(lows, highs))

    spans = lax.fori_loop(0, tokens.bit_length(), halve, tuple((jnp.int32(0), first) for first in firsts))
    starts = [lo for lo, _ in spans]
    for n in range(own_blocks):
        start_s[n] = starts[n]
    lane = lax.broadcasted_iota(jnp.int32, (own_blocks, BLK), 1)
    docs = jnp.concatenate([doc2_ref[pl.ds(b, 1), :] for b in packed], axis=0)
    opens = (lane > 0) & (docs != pltpu.roll(docs, 1, 1))
    first_of = jnp.concatenate([jnp.full((1, BLK), first, jnp.int32) for first in firsts], axis=0)
    start_of = jnp.concatenate([jnp.full((1, BLK), start, jnp.int32) for start in starts], axis=0)
    begin = jnp.where(opens, first_of + lane, start_of)
    step = 1
    while step < BLK:
        begin = jnp.maximum(begin, jnp.where(lane >= step, pltpu.roll(begin, step, 1), 0))
        step *= 2
    begin_s[...] = begin
    pltpu.make_async_copy(kv_ref, kv_s.at[:, pl.ds(FRONT, tokens)], sem.at[0]).wait()

    def turn(i, carry):
        at = pl.ds(pl.multiple_of(FRONT + i * turned, BLK), turned)
        kvt_s[0, :, at] = dot(eye_d, kv_s[0, at, :], NT).astype(BF16)
        kvt_s[1, :, at] = dot(eye_d, kv_s[1, at, :], NT).astype(BF16)
        return carry

    lax.fori_loop(0, tokens // turned, turn, 0)

    def query_block(n, carry):
        packed = order_ref[plane_ref[0] * own_blocks + n]
        first = packed * BLK
        doc_start = start_s[n]
        pairs = (first // BLK - doc_start // BLK + PAIR // BLK) // (PAIR // BLK)
        base = FRONT + first + BLK - pairs * PAIR
        lead = (pairs - 1) % (KTILE // PAIR) + 1
        tiles = (pairs - 1) // (KTILE // PAIR)

        def each_tile(work):
            for size in range(1, KTILE // PAIR + 1):
                @pl.when(lead == size)
                def _():
                    work(0, size * PAIR, True)

            def step(t, carry):
                work(pl.multiple_of(lead * PAIR + t * KTILE, PAIR), KTILE, False)
                return carry

            lax.fori_loop(0, tiles, step, 0)

        begin = begin_s[pl.ds(n, 1), :]
        lane = lax.broadcasted_iota(jnp.int32, (1, BLK), 1)
        bias = jnp.where(begin > doc_start, NEG, 0.0)
        bias = jnp.concatenate([bias] * heads, axis=1)
        low = jnp.concatenate([begin] * heads, axis=1) + (FRONT - base)
        high = jnp.concatenate([first + lane] * heads, axis=1) + (FRONT - base)

        here = aligned(n, BLK)
        qs = jnp.concatenate([q_s[here, h * HD:(h + 1) * HD] for h in range(heads)], axis=0)
        gs = jnp.concatenate([g_s[here, h * HD:(h + 1) * HD] for h in range(heads)], axis=0)

        def score_tile(rel, width, leads):
            score = dot(kv_s[0, pl.ds(pl.multiple_of(base + rel, BLK), width), :], qs, NT)
            cuts = [(0, PAIR, True)] if leads else []
            if leads and width > PAIR:
                cuts += [(PAIR, width - BLK, False), (width - BLK, width, True)]
            elif not leads:
                cuts = [(0, width - BLK, False), (width - BLK, width, True)]
            top = None
            for start, end, edge in cuts:
                count = end - start
                part = score[start:end] * (SCALE * LOG2E)
                if edge:
                    key_at = lax.broadcasted_iota(jnp.int32, (count, rows), 0)
                    seen = (key_at >= low - (rel + start)) & (key_at <= high - (rel + start))
                    part = jnp.where(seen, part, NEG)
                else:
                    part = part + bias
                s_s[pl.ds(pl.multiple_of(rel + start, BLK), count), :] = part
                most = jnp.max(part.reshape(count // LANES, LANES, rows), axis=0)
                top = most if top is None else jnp.maximum(top, most)
            top_s[...] = top if leads else jnp.maximum(top_s[...], top)

        each_tile(score_tile)
        top = jnp.max(top_s[...], axis=0, keepdims=True)

        def prob_tile(rel, width, leads):
            at = pl.ds(pl.multiple_of(base + rel, BLK), width)
            there = pl.ds(pl.multiple_of(rel, PAIR), width)
            prob = jnp.exp2(s_s[there, :] - top)
            rounded = prob.astype(BF16)
            p_s[there, :] = rounded
            part = dot(kvt_s[1, :, at], rounded, NN)
            total = jnp.sum(prob.reshape(width // LANES, LANES, rows), axis=0)
            if leads:
                acc_s[...] = part
                total_s[...] = total
            else:
                acc_s[...] += part
                total_s[...] += total

        each_tile(prob_tile)
        inverse = 1.0 / jnp.sum(total_s[...], axis=0, keepdims=True)
        att_t = (acc_s[...] * inverse).astype(BF16)
        g_t = dot(eye_d, gs, NT)
        q_t = dot(eye_d, qs, NT)
        delta = jnp.sum(g_t * att_t.astype(F32), axis=0, keepdims=True)
        g_n = (g_t * inverse).astype(BF16)
        q_n = (q_t * (inverse * SCALE)).astype(BF16)
        att = dot(eye_r, att_t, NT).astype(BF16)
        for h in range(heads):
            att_s[here, h * HD:(h + 1) * HD] = att[h * BLK:(h + 1) * BLK]

        def grad_tile(rel, width, leads):
            at = pl.ds(pl.multiple_of(base + rel, BLK), width)
            prob = p_s[pl.ds(pl.multiple_of(rel, PAIR), width), :]
            dprob = dot(kv_s[1, at, :], gs, NT)
            dscore = (prob.astype(F32) * (dprob - delta)).astype(BF16)
            dkv_s[1, at, :] += dot(prob, g_n, NT)
            dkv_s[0, at, :] += dot(dscore, q_n, NT)
            part = dot(kvt_s[0, :, at], dscore, NN)
            if leads:
                acc_s[...] = part
            else:
                acc_s[...] += part

        each_tile(grad_tile)
        dq_t = (acc_s[...] * (inverse * SCALE)).astype(BF16)
        dq = dot(eye_r, dq_t, NT).astype(BF16)
        for h in range(heads):
            dq_s[here, h * HD:(h + 1) * HD] = dq[h * BLK:(h + 1) * BLK]
        pltpu.make_async_copy(att_s.at[here], att_ref.at[here], sem.at[2]).start()
        pltpu.make_async_copy(dq_s.at[here], dq_ref.at[here], sem.at[3]).start()
        return carry

    load_q.wait()
    load_g.wait()
    lax.fori_loop(0, own_blocks, query_block, 0)

    def hand_out(i, carry):
        for j in range(OUT):
            src = pl.ds(pl.multiple_of(FRONT + order_ref[i * OUT + j] * BLK, BLK), BLK)
            dst = aligned(i * OUT + j, BLK)
            out_s[:, dst, :] = dkv_s[:, src, :].astype(BF16)
        dst = aligned(i, OUT * BLK)
        pltpu.make_async_copy(out_s.at[:, dst], dkv_ref.at[:, dst], sem.at[1]).start()
        return carry

    lax.fori_loop(0, blocks // OUT, hand_out, 0)
    pltpu.make_async_copy(att_s, att_ref, sem.at[2]).wait()
    pltpu.make_async_copy(dq_s, dq_ref, sem.at[3]).wait()
    pltpu.make_async_copy(out_s, dkv_ref, sem.at[1]).wait()


def attend(plane, q_loc, g_loc, kv, doc_ids, block_order):
    tokens = kv.shape[1]
    rows = q_loc.shape[1] // HD * BLK
    padded = FRONT + tokens
    longest = (min(tokens, 4096) + BLK + PAIR - 1) // PAIR * PAIR
    vmem = pl.BlockSpec(memory_space=pltpu.VMEM)
    smem = pl.BlockSpec(memory_space=pltpu.SMEM)
    any_space = pl.BlockSpec(memory_space=pl.ANY)
    return pl.pallas_call(
        attend_kernel,
        out_shape=(
            jax.ShapeDtypeStruct(q_loc.shape, BF16),
            jax.ShapeDtypeStruct(q_loc.shape, BF16),
            jax.ShapeDtypeStruct(kv.shape, BF16),
        ),
        in_specs=[smem, smem, smem, vmem, any_space, any_space, any_space],
        out_specs=(any_space,) * 3,
        scratch_shapes=[
            pltpu.VMEM(q_loc.shape, BF16),
            pltpu.VMEM(q_loc.shape, BF16),
            pltpu.VMEM(q_loc.shape, BF16),
            pltpu.VMEM(q_loc.shape, BF16),
            pltpu.VMEM((2, padded, HD), BF16),
            pltpu.VMEM((2, HD, padded), BF16),
            pltpu.VMEM((2, padded, HD), F32),
            pltpu.VMEM((2, tokens, HD), BF16),
            pltpu.VMEM((longest, rows), F32),
            pltpu.VMEM((longest, rows), BF16),
            pltpu.VMEM((HD, rows), F32),
            pltpu.VMEM((LANES, rows), F32),
            pltpu.VMEM((LANES, rows), F32),
            pltpu.VMEM((q_loc.shape[0] // BLK, BLK), jnp.int32),
            pltpu.SMEM((q_loc.shape[0] // BLK,), jnp.int32),
            pltpu.SemaphoreType.DMA((4,)),
        ],
        compiler_params=pltpu.CompilerParams(vmem_limit_bytes=VMEM_LIMIT),
        name="attend",
    )(block_order, doc_ids, plane, doc_ids.reshape(tokens // BLK, BLK), q_loc, g_loc, kv)


def scatter_kernel(planes, groups, att_ref, dq_ref, dkv_ref, ao_ref, dqo_ref, land_s,
                   mine_s, sib_s, stage_s, came_s, fin_s,
                   local, mine_sem, sib_send, sib_recv, a2a_send, a2a_recv, z_send, z_recv):
    at = Where(planes, groups)
    rows = ao_ref.shape[0]
    wide = att_ref.shape[1]
    piece_rows = dkv_ref.shape[2] // PIECES
    hops = planes // 2
    mine = aligned(at.p, rows)
    cols = aligned(at.g * NS + at.s, wide)

    own_a = pltpu.make_async_copy(att_ref.at[mine], ao_ref.at[:, cols], local.at[0])
    own_q = pltpu.make_async_copy(dq_ref.at[mine], dqo_ref.at[:, cols], local.at[1])
    own_a.start()
    own_q.start()

    turns = [hops]
    for j in range(hops - 1, 0, -1):
        turns += [j, -j]
    turns += [0]
    own_part, sib_part = [], []
    for n, distance in enumerate(turns):
        chunk = (at.z + planes + distance) % planes
        own_part.append(pltpu.make_async_copy(dkv_ref.at[at.core, chunk], mine_s.at[chunk], mine_sem.at[n]))
        sib_part.append(remote(dkv_ref.at[1 - at.core, chunk], sib_s.at[chunk],
                               sib_send.at[n], sib_recv.at[n], at.sib))
    for copy in own_part:
        copy.start()
    at.greet()
    for copy in sib_part:
        copy.start()

    def send_out(os, og, device):
        theirs = aligned(os * groups + og, rows)
        remote(att_ref.at[theirs], ao_ref.at[:, cols], a2a_send.at[0], a2a_recv.at[0], device).start()
        remote(dq_ref.at[theirs], dqo_ref.at[:, cols], a2a_send.at[1], a2a_recv.at[1], device).start()

    def ready(distance):
        n = turns.index(distance)
        own_part[n].wait()
        sib_part[n].wait_recv()

    def own_sum(distance, half):
        chunk = (at.z + planes + distance) % planes
        part = pl.ds(half * piece_rows, piece_rows)
        return mine_s[chunk, part, :].astype(F32) + sib_s[chunk, part, :].astype(F32)

    def moves(j, half, way):
        return j > 0 or half * 2 // PIECES == way

    def send(j, half, way):
        slot = (way, PIECES * j + half)
        return remote(stage_s.at[slot], came_s.at[slot], z_send.at[slot], z_recv.at[slot],
                      at.up if way == 0 else at.down)

    for j in range(hops):
        distance = hops - j
        if j == 0:
            ready(hops)
        else:
            ready(distance)
            ready(-distance)
        for turn in range(PIECES):
            for way in (0, 1):
                half = (turn + (1 - way) * PIECES // 2) % PIECES
                if not moves(j, half, way):
                    continue
                value = own_sum(distance if way == 0 else -distance, half)
                if j > 0 and moves(j - 1, half, way):
                    send(j - 1, half, way).wait_recv()
                    value = value + came_s[way, PIECES * (j - 1) + half].astype(F32)
                stage_s[way, PIECES * j + half] = value.astype(BF16)
                send(j, half, way).start()
        if j == OUT_AT:
            at.each_peer(send_out)

    ready(0)
    for half in range(PIECES):
        value = own_sum(0, half)
        for way in (0, 1):
            if moves(hops - 1, half, way):
                send(hops - 1, half, way).wait_recv()
                value = value + came_s[way, PIECES * (hops - 1) + half].astype(F32)
        fin_s[pl.ds(half * piece_rows, piece_rows), :] = value.astype(BF16)

    group_cols = aligned(at.g, HD)
    target = land_s.at[at.core, at.ylo, :, group_cols]
    own_fin = pltpu.make_async_copy(fin_s.at[mine], target, local.at[2])
    own_fin.start()

    for a in range(NS):
        for os, og, device in at.peers(a):
            remote(fin_s.at[aligned(os * groups + og, rows)], target, a2a_send.at[2], a2a_recv.at[2], device).start()

    others = pl.ds(0, rows * (at.size - 1))
    some = pl.ds(0, wide * (at.size - 1))
    own_a.wait()
    own_q.wait()
    for n, (src, dst) in enumerate(((att_ref, ao_ref), (dq_ref, dqo_ref))):
        sent, came = src.at[others], dst.at[:, some]
        remote(came, came, a2a_send.at[n], a2a_recv.at[n], at.up).wait_recv()
        remote(sent, sent, a2a_send.at[n], a2a_recv.at[n], at.up).wait_send()
    for j in range(hops):
        for half in range(PIECES):
            for way in (0, 1):
                if moves(j, half, way):
                    send(j, half, way).wait_send()
    for copy in sib_part:
        copy.wait_send()
    own_fin.wait()
    moved = fin_s.at[others]
    remote(moved, moved, a2a_send.at[2], a2a_recv.at[2], at.up).wait()


def scatter(planes, groups, att, dq, dkv):
    plane_rows = att.shape[0]
    rows = plane_rows // (NS * groups)
    columns = att.shape[1] * NS * groups
    hops = planes // 2
    any_space = pl.BlockSpec(memory_space=pl.ANY)
    dma = pltpu.SemaphoreType.DMA
    return pl.pallas_call(
        functools.partial(scatter_kernel, planes, groups),
        out_shape=(
            jax.ShapeDtypeStruct((rows, columns), BF16),
            jax.ShapeDtypeStruct((rows, columns), BF16),
            jax.ShapeDtypeStruct((2, NS // 2, rows, groups * HD), BF16),
        ),
        in_specs=[any_space] * 3,
        out_specs=(any_space,) * 3,
        scratch_shapes=[
            pltpu.VMEM((planes, plane_rows, HD), BF16),
            pltpu.VMEM((planes, plane_rows, HD), BF16),
            pltpu.VMEM((2, PIECES * hops, plane_rows // PIECES, HD), BF16),
            pltpu.VMEM((2, PIECES * hops, plane_rows // PIECES, HD), BF16),
            pltpu.VMEM((plane_rows, HD), BF16),
            dma((3,)),
            dma((planes,)),
            dma((planes,)),
            dma((planes,)),
            dma((3,)),
            dma((3,)),
            dma((2, PIECES * hops)),
            dma((2, PIECES * hops)),
        ],
        compiler_params=pltpu.CompilerParams(
            collective_id=1, has_side_effects=True, vmem_limit_bytes=VMEM_LIMIT
        ),
        name="scatter",
    )(att, dq, dkv)


def finish_kernel(a_ref, q_ref, land_ref, ao_ref, qo_ref, kg_ref, vg_ref, sem):
    moves = [pltpu.make_async_copy(a_ref, ao_ref, sem.at[0]), pltpu.make_async_copy(q_ref, qo_ref, sem.at[1])]
    for move in moves:
        move.start()
    for part, out in ((0, kg_ref), (1, vg_ref)):
        total = land_ref[part, 0].astype(F32)
        for ylo in range(1, NS // 2):
            total = total + land_ref[part, ylo].astype(F32)
        out[...] = total.astype(BF16)
    for move in moves:
        move.wait()


def finish(att, dq, land):
    any_space = pl.BlockSpec(memory_space=pl.ANY)
    vmem = pl.BlockSpec(memory_space=pltpu.VMEM)
    grad = jax.ShapeDtypeStruct(land.shape[2:], BF16)
    return pl.pallas_call(
        finish_kernel,
        out_shape=(jax.ShapeDtypeStruct(att.shape, BF16), jax.ShapeDtypeStruct(dq.shape, BF16), grad, grad),
        in_specs=[vmem, vmem, vmem],
        out_specs=(any_space, any_space, vmem, vmem),
        scratch_shapes=[pltpu.SemaphoreType.DMA((2,))],
        name="finish",
    )(att, dq, land)


def per_device(planes, groups, queries, keys, values, out_grad, doc_ids, block_order):
    plane = (lax.axis_index("ctx") // NS).astype(jnp.int32).reshape(1)
    q_loc, g_loc, kv = gather(planes, groups, queries, keys, values, out_grad)
    tokens = doc_ids.shape[0]
    att, dq, dkv = attend(plane, q_loc, g_loc, kv.reshape(2, tokens, HD), doc_ids, block_order)
    return finish(*scatter(planes, groups, att, dq, dkv.reshape(kv.shape)))


def solution(mesh):
    split = P(("ctx", "head"), None)
    planes, groups = mesh.shape["ctx"] // NS, mesh.shape["head"]
    return jax.shard_map(
        functools.partial(per_device, planes, groups),
        mesh=mesh,
        in_specs=(split, split, split, split, P(), P()),
        out_specs=(split, split, split, split),
        check_vma=False,
    )
```
